32 devices in a mesh: groups: 2 (over x), batch: 8 (over z, y), tensor: 2 (over core).
Axes of the slice: x: 2, y: 2, z: 4, core: 2. Of those that a mesh axis runs over, the one named last changes fastest.
Arguments:
- tokens: bfloat16 [256, 5120], P(('groups', 'batch'), 'tensor'), parts along dimension 0, may hold values from -6 to 6
- gate_weight: bfloat16 [5120, 13824], P(None, ('batch', 'tensor')), may hold values from -0.078125 to 0.078125
- up_weight: bfloat16 [5120, 13824], P(None, ('batch', 'tensor')), may hold values from -0.078125 to 0.078125
- down_weight: bfloat16 [13824, 5120], P(('batch', 'tensor')), may hold values from -0.0546875 to 0.0546875
- adapter_in: bfloat16 [32, 64, 13824], P('groups', None, ('batch', 'tensor')), parts along dimension 0, may hold values from -0.0546875 to 0.0546875
- adapter_out: bfloat16 [32, 64, 5120], P('groups', None, ('batch', 'tensor')), parts along dimension 0, may hold values from -0.75 to 0.75
- cotangent: bfloat16 [256, 5120], P('groups', ('batch', 'tensor')), parts along dimension 0, may hold values from -6 to 6
- block_owner: int32 [4], P('groups'), parts along dimension 0, may hold values from 0 to 15
- block_length: int32 [4], P('groups'), parts along dimension 0, may hold values from 1 to 64
- placement: int32 [32], P('groups'), parts along dimension 0, may hold values from 0 to 15, each once
Outputs:
- mixed: bfloat16 [256, 5120], P('groups', ('batch', 'tensor')), parts along dimension 0
- grad_in: bfloat16 [32, 64, 13824], P(('groups', 'batch', 'tensor')), parts along dimension 0
- grad_out: bfloat16 [32, 64, 5120], P(('groups', 'batch', 'tensor')), parts along dimension 0
The draws below stay inside these ranges and needn't reach their ends.
There are 2 independent parts, one for each index of `groups`. The reference program is written for one: setup_inputs(seed, part) draws one part's arguments, and reference() takes and returns one part's arrays. A program takes and returns all parts, laid end to end along the dimension named above; an argument that names none is the same for every part. Nothing has to cross between parts.
Inputs may be any that keep to these rules, and one draw needn't show every extreme that they name: `block_owner`: owner of each block of 64 tokens; some owners have no block. `block_length`: padded tokens lie at the end of each block. `placement`: a permutation; slot j belongs to the j-th device of batch+tensor.
All inputs are finite; a program needn't handle non-finite values.
Results may differ from the reference program's by a relative error of at most 0.0085.
Values may be sent and summed in bfloat16 or wider, within the bound.
No kernel may reach another device: no remote copies, remote signals or barrier semaphores. Data moves between devices by JAX's collectives and lax.ppermute only.
A program may use at most 128 MiB of HBM per device.

```python
import math
import jax
import jax.numpy as jnp
import numpy as np
from jax import lax

D = 5120
FF = 13824
RANK = 64
BLOCK = 64
TOKENS = 128
BLOCKS = 2
OWNERS = 16
N_BATCH = 8


def levels(stream_key, dims, pieces, smallest, top_value):
    def one(dim, blocks):
        steps = jax.random.uniform(jax.random.fold_in(jax.random.fold_in(stream_key, 6), dim), (blocks,), jnp.float32, smallest / len(pieces), top_value / len(pieces))
        return jnp.repeat(jnp.exp(steps), dims[dim] // blocks).reshape((-1,) + (1,) * (len(dims) - dim - 1))

    level = one(*pieces[0])
    for cut in pieces[1:]:
        level = level * one(*cut)
    return level


def rank_table(amount, skew):
    weights = [(1 << 20) // math.isqrt(rank ** skew) + 1 for rank in range(1, amount + 1)]
    scale = 1 + sum(weights) // (1 << 30)
    return np.cumsum(np.array([max(1, weight // scale) for weight in weights]))


def ranked_ids(stream_key, shape, amount, slope):
    grid = rank_table(amount, slope)
    pick = jax.random.randint(jax.random.fold_in(stream_key, 1), shape, 0, int(grid[amount - 1]))
    standing = jnp.searchsorted(jnp.asarray(grid, jnp.int32), pick, side="right")
    return jax.random.permutation(jax.random.fold_in(stream_key, 2), amount)[standing].astype(jnp.int32)


def scatter_about(stream_key, shape, scale, limit, pieces=(), kind=jnp.bfloat16):
    drawn = scale * jax.random.normal(stream_key, shape, jnp.float32)
    if pieces:
        drawn = drawn * levels(stream_key, shape, pieces, -0.22, 0.18)
    return jnp.clip(drawn, -limit, limit).astype(kind)


def setup_inputs(seed: int = 0, part: int = 0) -> dict:
    streams_of = jax.random.split(jax.random.key(seed), 11)
    own_keys = jax.random.split(jax.random.fold_in(streams_of[10], part), 11)
    tokens = scatter_about(own_keys[0], (TOKENS, D), 1.0, 6.0, ((0, 8), (1, 2)))
    gate_weight = scatter_about(streams_of[1], (D, FF), D ** -0.5, 0.078125, ((1, 16),))
    up_weight = scatter_about(streams_of[2], (D, FF), D ** -0.5, 0.078125, ((1, 16),))
    down_weight = scatter_about(streams_of[3], (FF, D), FF ** -0.5, 0.0546875, ((0, 16),))
    adapter_in = scatter_about(own_keys[4], (OWNERS, RANK, FF), FF ** -0.5, 0.0546875, ((2, 16),))
    adapter_out = scatter_about(own_keys[5], (OWNERS, RANK, D), RANK ** -0.5, 0.75, ((2, 16),))
    cotangent = scatter_about(own_keys[6], (TOKENS, D), 1.0, 6.0, ((1, 16),))
    block_owner = ranked_ids(own_keys[7], (BLOCKS,), OWNERS, 2)
    block_length = jax.random.randint(own_keys[8], (BLOCKS,), 1, BLOCK + 1).astype(jnp.int32)
    placement = jax.random.permutation(own_keys[9], OWNERS).astype(jnp.int32)
    return {"tokens": tokens, "gate_weight": gate_weight, "up_weight": up_weight, "down_weight": down_weight, "adapter_in": adapter_in, "adapter_out": adapter_out, "cotangent": cotangent, "block_owner": block_owner, "block_length": block_length, "placement": placement}


lowrank_adapter_scale = 2.0


def reference(tokens, gate_weight, up_weight, down_weight, adapter_in, adapter_out, cotangent, block_owner, block_length, placement):
    highest = lax.Precision.HIGHEST
    gate_value = jnp.dot(tokens, gate_weight, preferred_element_type=jnp.float32)
    up_value = jnp.dot(tokens, up_weight, preferred_element_type=jnp.float32)
    hidden = (jax.nn.silu(gate_value) * up_value).astype(jnp.bfloat16)
    group_count = N_BATCH
    group_width = FF // group_count
    hidden_groups = hidden.reshape(TOKENS, group_count, group_width).transpose(1, 0, 2)
    down_groups = down_weight.reshape(group_count, group_width, D)

    def add_group(total, pair):
        term = jnp.dot(pair[0], pair[1], preferred_element_type=jnp.float32).astype(jnp.bfloat16)
        term = lax.optimization_barrier(term)
        return total + term.astype(jnp.float32), None

    frozen_base_total, _ = lax.scan(add_group, jnp.zeros((TOKENS, D), jnp.float32), (hidden_groups, down_groups))
    in_blocks = adapter_in[block_owner].astype(jnp.float32)
    out_blocks = adapter_out[block_owner].astype(jnp.float32)
    hidden_blocks = hidden.reshape(BLOCKS, BLOCK, FF)
    position = lax.broadcasted_iota(jnp.int32, (BLOCKS, BLOCK), 1)
    live_mask = (position < block_length[:, None]).astype(jnp.bfloat16)
    masked = cotangent.reshape(BLOCKS, BLOCK, D) * live_mask[:, :, None]
    low_sum = jnp.einsum("bsf,brf->bsr", hidden_blocks.astype(jnp.float32), in_blocks, precision=highest)
    back_sum = jnp.einsum("bsd,brd->bsr", masked.astype(jnp.float32), out_blocks, precision=highest)
    low = low_sum.astype(jnp.bfloat16)
    back = back_sum.astype(jnp.bfloat16)
    adapter_contribution = jnp.einsum("bsr,brd->bsd", low.astype(jnp.float32), out_blocks, precision=highest).reshape(TOKENS, D)
    mixed = (frozen_base_total + lowrank_adapter_scale * adapter_contribution).astype(jnp.bfloat16)
    owner_indicator = (jnp.arange(OWNERS, dtype=jnp.int32)[:, None] == block_owner[None, :]).astype(jnp.float32)
    owner_token_counts = jnp.dot(owner_indicator, block_length.astype(jnp.float32), precision=highest)
    coefficient = owner_indicator * (lowrank_adapter_scale / jnp.maximum(owner_token_counts, 1.0))[:, None]
    out_terms = jnp.einsum("bsr,bsd->brd", low.astype(jnp.float32), masked.astype(jnp.float32), precision=highest)
    in_terms = jnp.einsum("bsr,bsf->brf", back.astype(jnp.float32), hidden_blocks.astype(jnp.float32), precision=highest)
    owner_out = jnp.einsum("ob,brd->ord", coefficient, out_terms, precision=highest)
    owner_in = jnp.einsum("ob,brf->orf", coefficient, in_terms, precision=highest)
    grad_in = owner_in[placement].astype(jnp.bfloat16)
    grad_out = owner_out[placement].astype(jnp.bfloat16)
    return mixed, grad_in, grad_out
```

```python
import jax
import jax.numpy as jnp
from jax import lax
from jax.sharding import PartitionSpec as P

lowrank_adapter_scale = 2.0


def partner_shifts(count):
    return [[(i, i ^ k) for i in range(count)] for k in range(1, count)]


def gather_pieces(piece, axis):
    count = lax.axis_size(axis)
    if count & (count - 1) or count > 8:
        return lax.all_gather(piece, axis)
    me = lax.axis_index(axis)
    whole = jnp.zeros((count,) + piece.shape, piece.dtype)
    whole = lax.dynamic_update_index_in_dim(whole, piece, me, 0)
    for k, pairs in enumerate(partner_shifts(count), 1):
        arrived = lax.ppermute(piece, axis, pairs)
        whole = lax.dynamic_update_index_in_dim(whole, arrived, me ^ k, 0)
    return whole


def exchange_sum(pieces, axis):
    count = lax.axis_size(axis)
    if count & (count - 1) or count > 8:
        arrived = lax.all_to_all(pieces, axis, split_axis=0, concat_axis=0, tiled=True)
        return arrived.astype(jnp.float32).sum(0)
    me = lax.axis_index(axis)
    total = lax.dynamic_index_in_dim(pieces, me, 0, keepdims=False).astype(jnp.float32)
    for k, pairs in enumerate(partner_shifts(count), 1):
        leaving = lax.dynamic_index_in_dim(pieces, me ^ k, 0, keepdims=False)
        total = total + lax.ppermute(leaving, axis, pairs).astype(jnp.float32)
    return total


def pair_gather(piece):
    count = lax.axis_size("tensor")
    if count != 2:
        return lax.all_gather(piece, "tensor")
    other = lax.ppermute(piece, "tensor", [(0, 1), (1, 0)])
    mine_first = lax.axis_index("tensor") == 0
    return jnp.stack([jnp.where(mine_first, piece, other), jnp.where(mine_first, other, piece)])


def on_device(
    tokens,
    gate_weight,
    up_weight,
    down_weight,
    adapter_in,
    adapter_out,
    cotangent,
    block_owner,
    block_length,
    placement,
):
    f32, bf16 = jnp.float32, jnp.bfloat16
    batch_count, tensor_count = lax.axis_size("batch"), lax.axis_size("tensor")
    core = lax.axis_index("tensor")
    width = gate_weight.shape[1]
    model_width = gate_weight.shape[0]
    columns = cotangent.shape[1]
    token_count = cotangent.shape[0]
    block_count = block_owner.shape[0]
    block_size = token_count // block_count
    rank = adapter_in.shape[1]

    token_block = lax.broadcasted_iota(jnp.int32, (block_count, block_size), 0).reshape(-1)
    position = lax.broadcasted_iota(jnp.int32, (block_count, block_size), 1).reshape(-1)
    token_owner = jnp.repeat(block_owner, block_size)
    live = position < jnp.repeat(block_length, block_size)
    own_block = lax.broadcasted_iota(jnp.int32, (block_count, 1, 1), 0) == token_block

    def in_rank_space(matrices, features):
        every = jnp.dot(
            matrices.reshape(block_count * rank, -1), features, preferred_element_type=f32
        )
        return jnp.where(own_block, every.reshape(block_count, rank, token_count), 0.0).sum(0)

    in_blocks = adapter_in[block_owner]
    out_blocks = adapter_out[block_owner]
    cot_t = cotangent.T
    half = gather_pieces(tokens, "batch").reshape(token_count, -1)
    halves = pair_gather(half)
    rows = jnp.concatenate([halves[c] for c in range(tensor_count)], axis=1)

    back_part = jnp.where(live, in_rank_space(out_blocks, cot_t), 0.0).astype(bf16)
    cot_all = gather_pieces(cot_t, "batch")

    def weights_first(weight, values):
        return lax.dot_general(
            weight, values, (((0,), (1,)), ((), ())), preferred_element_type=f32
        )

    gate_value = weights_first(gate_weight, rows)
    up_value = weights_first(up_weight, rows)
    hidden = (jax.nn.silu(gate_value) * up_value).astype(bf16)
    hidden_all = gather_pieces(hidden, "batch")

    low_part = in_rank_space(in_blocks, hidden)
    base_part = lax.dot_general(
        down_weight, hidden, (((0,), (0,)), ((), ())), preferred_element_type=f32
    ).astype(bf16)
    base_part = base_part.reshape(batch_count, tensor_count, columns, token_count)
    ranked = jnp.concatenate([low_part.astype(bf16), back_part], axis=0)
    if tensor_count == 2:
        leaving = lax.dynamic_index_in_dim(base_part, 1 - core, 1, keepdims=False)
        kept = lax.dynamic_index_in_dim(base_part, core, 1, keepdims=False)
        arrived, ranked_other = lax.ppermute((leaving, ranked), "tensor", [(0, 1), (1, 0)])
        chip_base = (kept.astype(f32) + arrived.astype(f32)).astype(bf16)
        chip_ranked = (ranked.astype(f32) + ranked_other.astype(f32)).astype(bf16)
    else:
        chip_base = lax.psum_scatter(base_part, "tensor", scatter_dimension=1)
        chip_ranked = lax.psum(ranked, "tensor")
    leaving = jnp.concatenate(
        [chip_base, jnp.broadcast_to(chip_ranked, (batch_count,) + chip_ranked.shape)], axis=1
    )
    total = exchange_sum(leaving, "batch")
    base_sum = total[:columns]
    low = total[columns : columns + rank].astype(bf16)
    back = total[columns + rank :].astype(bf16)

    spread = jnp.where(own_block, low[None], jnp.zeros((), bf16)).reshape(-1, token_count)
    contribution = lax.dot_general(
        out_blocks.reshape(block_count * rank, columns),
        spread,
        (((0,), (0,)), ((), ())),
        preferred_element_type=f32,
    )
    mixed = (base_sum + lowrank_adapter_scale * contribution).astype(bf16).T

    slot = lax.axis_index(("batch", "tensor"))
    owner = placement[slot]
    count = jnp.where(block_owner == owner, block_length, 0).sum().astype(f32)
    coefficient = lowrank_adapter_scale / jnp.maximum(count, 1.0)
    chosen = token_owner == owner
    low_chosen = jnp.where(chosen & live, low, jnp.zeros((), bf16))
    back_chosen = jnp.where(chosen, back, jnp.zeros((), bf16))

    def slot_grad(ranked_values, pieces):
        both = pair_gather(pieces)
        features = jnp.swapaxes(both, 0, 1).reshape(-1, token_count)
        grad = lax.dot_general(
            ranked_values, features, (((1,), (1,)), ((), ())), preferred_element_type=f32
        )
        return (coefficient * grad).astype(bf16)[None]

    return mixed, slot_grad(back_chosen, hidden_all), slot_grad(low_chosen, cot_all)


def solution(mesh):
    placed = (
        P(("groups", "batch"), "tensor"),
        P(None, ("batch", "tensor")),
        P(None, ("batch", "tensor")),
        P(("batch", "tensor"), None),
        P("groups", None, ("batch", "tensor")),
        P("groups", None, ("batch", "tensor")),
        P("groups", ("batch", "tensor")),
        P("groups"),
        P("groups"),
        P("groups"),
    )
    return jax.shard_map(
        on_device,
        mesh=mesh,
        in_specs=placed,
        out_specs=(
            P("groups", ("batch", "tensor")),
            P(("groups", "batch", "tensor"), None, None),
            P(("groups", "batch", "tensor"), None, None),
        ),
        check_vma=False,
    )
```

```python
import functools

import jax
import jax.numpy as jnp
from jax import lax
from jax.experimental import pallas as pl
from jax.experimental.pallas import tpu as pltpu
from jax.sharding import PartitionSpec as P

lowrank_adapter_scale = 2.0

ROWS_BY_ROWS = (((1,), (1,)), ((), ()))
GRAD_FLOPS = 20_000_000_000
IN_VMEM = pl.BlockSpec(memory_space=pltpu.VMEM)
IN_HBM = pl.BlockSpec(memory_space=pl.ANY)
IN_SMEM = pl.BlockSpec(memory_space=pltpu.SMEM)


def kernel_call(body, out_shape, in_specs, flops, moved, scratch=(), out_specs=None, limit=16):
    return pl.pallas_call(
        body,
        out_shape=out_shape,
        in_specs=in_specs,
        out_specs=jax.tree.map(lambda _: IN_VMEM, out_shape) if out_specs is None else out_specs,
        scratch_shapes=list(scratch),
        compiler_params=pltpu.CompilerParams(vmem_limit_bytes=limit << 20),
        cost_estimate=pl.CostEstimate(flops=flops, bytes_accessed=moved, transcendentals=0),
    )


def assemble_body(me, core, *refs):
    out = refs[-1]
    count = (len(refs) - 1) // 2
    rows, half = refs[0].shape
    for k in range(count):
        here = pl.ds(pl.multiple_of((me[0] ^ k) * rows, rows), rows)
        out[here, pl.ds(pl.multiple_of(core[0] * half, 128), half)] = refs[k][...]
        out[here, pl.ds(pl.multiple_of((1 - core[0]) * half, 128), half)] = refs[count + k][...]


def token_facts(block_count, token_count):
    lane = lax.broadcasted_iota(jnp.int32, (1, token_count), 1)
    size = token_count // block_count
    return [(lane >= b * size) & (lane < (b + 1) * size) for b in range(block_count)], lane, size


def live_mask(length, block_count, token_count):
    blocks, lane, size = token_facts(block_count, token_count)
    live = jnp.zeros((1, token_count), jnp.bool_)
    for b in range(block_count):
        live = live | (blocks[b] & (lane < b * size + length[b]))
    return live


def chosen_mask(owner, mine, block_count, token_count):
    blocks, lane, _ = token_facts(block_count, token_count)
    first = lane < 0
    for b in range(block_count):
        first = first | (blocks[b] & (lane < jnp.where(owner[b] == mine, token_count, 0)))
    return first


def back_body(owner, length, adapter_out, cot, out):
    block_count, token_count = owner.shape[0], cot.shape[1]
    blocks, _, _ = token_facts(block_count, token_count)
    columns = cot.shape[0]
    out[:columns] = cot[...]
    total = jnp.zeros((adapter_out.shape[1], token_count), jnp.float32)
    for b in range(block_count):
        every = jnp.dot(adapter_out[owner[b]], cot[...], preferred_element_type=jnp.float32)
        total = jnp.where(blocks[b], every, total)
    total = jnp.where(live_mask(length, block_count, token_count), total, 0.0)
    out[columns:] = total.astype(out.dtype)


def split_body(owner, core, base, hidden, adapter_in, kept, leaving):
    block_count, token_count = owner.shape[0], base.shape[0]
    rank = adapter_in.shape[1]
    columns = (kept.shape[0] - rank) // 8
    for b in range(8):
        both = base[:, b * 2 * columns : (b + 1) * 2 * columns].astype(jnp.float32).T
        both = both.astype(kept.dtype)
        here = pl.ds(b * columns, columns)

        @pl.when(core[0] == 0)
        def _():
            kept[here] = both[:columns]
            leaving[here] = both[columns:]

        @pl.when(core[0] != 0)
        def _():
            kept[here] = both[columns:]
            leaving[here] = both[:columns]

    blocks, _, _ = token_facts(block_count, token_count)
    low = jnp.zeros((rank, token_count), jnp.float32)
    for b in range(block_count):
        every = jnp.dot(adapter_in[owner[b]], hidden[...], preferred_element_type=jnp.float32)
        low = jnp.where(blocks[b], every, low)
    tail = pl.ds(8 * columns, rank)
    kept[tail] = low.astype(kept.dtype)
    leaving[tail] = low.astype(kept.dtype)


def add_body(me, kept, arrived, own, leaving):
    rank = own.shape[0] - (kept.shape[0] - own.shape[0])
    columns = (own.shape[0] - rank) // 4
    side = me[0] % 2

    def added(first, count):
        here = pl.ds(first, count)
        total = kept[here].astype(jnp.float32) + arrived[here].astype(jnp.float32)
        return total.astype(own.dtype)

    for z in range(4):
        here = pl.ds(z * columns, columns)
        own[here] = added(pl.multiple_of((2 * z + side) * columns, 16), columns)
        leaving[here] = added(pl.multiple_of((2 * z + 1 - side) * columns, 16), columns)
    low = added(8 * columns, rank)
    own[4 * columns :] = low
    leaving[4 * columns :] = low


def add_pair_body(me, own, arrived, *refs):
    outs = refs[-4:]
    columns = (own.shape[0] - outs[0].shape[0]) // 3
    place = me[0] // 2

    def added(first, count):
        here = pl.ds(first, count)
        total = own[here].astype(jnp.float32) + arrived[here].astype(jnp.float32)
        return total.astype(own.dtype)

    low = added(4 * columns, own.shape[0] - 4 * columns)
    for flip, out in enumerate(outs):
        out[:columns] = added(pl.multiple_of((place ^ flip) * columns, 16), columns)
        out[columns:] = low


def final_body(owner, length, mine, adapter_out, *refs):
    arrived, (mixed, ranked) = refs[:-2], refs[-2:]
    block_count, token_count = owner.shape[0], mixed.shape[1]
    columns = mixed.shape[0]
    total = arrived[0][...].astype(jnp.float32)
    for share in arrived[1:]:
        total = total + share[...].astype(jnp.float32)
    low = total[columns:]
    blocks, _, _ = token_facts(block_count, token_count)
    contribution = jnp.zeros(mixed.shape, jnp.float32)
    for b in range(block_count):
        every = lax.dot_general(
            adapter_out[owner[b]],
            low.astype(jnp.bfloat16),
            (((0,), (0,)), ((), ())),
            preferred_element_type=jnp.float32,
        )
        contribution = jnp.where(blocks[b], every, contribution)
    mixed[...] = (total[:columns] + lowrank_adapter_scale * contribution).astype(mixed.dtype)
    chosen = chosen_mask(owner, mine[0], block_count, token_count)
    live = live_mask(length, block_count, token_count)
    ranked[...] = jnp.where(chosen & live, low, 0.0).astype(ranked.dtype)


def stack_body(me, *refs):
    out = refs[-1]
    for flip, piece in enumerate(refs[:-1]):
        out[(me[0] // 2) ^ flip] = piece[...]


def interleave_body(me, near, far, out):
    side = me[0] % 2
    for z in range(near.shape[0]):
        out[2 * z + side] = near[z]
        out[2 * z + 1 - side] = far[z]


def gathered_body(owner, mine, core, gathered, gathered_other, features, ranked):
    columns = features.shape[0] // (2 * gathered.shape[0])
    back = jnp.zeros(ranked.shape, jnp.float32)
    for half, pieces in ((core[0], gathered), (1 - core[0], gathered_other)):
        for b in range(pieces.shape[0]):
            here = pl.ds(pl.multiple_of((2 * b + half) * columns, 16), columns)
            features[here] = pieces[b, :columns]
            back = back + pieces[b, columns:].astype(jnp.float32)
    chosen = chosen_mask(owner, mine[0], owner.shape[0], ranked.shape[1])
    ranked[...] = jnp.where(chosen, back, 0.0).astype(ranked.dtype)


def coefficient_of(owner, length, mine):
    count = jnp.int32(0)
    for b in range(owner.shape[0]):
        count = count + jnp.where(owner[b] == mine[0], length[b], 0)
    return lowrank_adapter_scale / jnp.maximum(count, 1).astype(jnp.float32)


def grad_of_array_body(owner, length, mine, ranked, features, out):
    total = lax.dot_general(
        ranked[...], features[...], ROWS_BY_ROWS, preferred_element_type=jnp.float32
    )
    out[0] = (coefficient_of(owner, length, mine) * total).astype(out.dtype)


def grad_of_pieces_body(owner, length, mine, me, ranked, *refs, flips):
    near, near_other, far, far_other = refs[:4]
    out, features, result, sems = refs[-4:]
    rows = near.shape[0]
    chip, core = (me[0] ^ flips) // 2, me[1]
    lower = me[0] % 2
    copies = []
    for k, piece in enumerate((near, near_other, far, far_other)):
        place = jnp.where(k < 2, lower, 1 - lower) * 2 + jnp.where(k % 2 == 0, core, 1 - core)
        here = pl.ds(pl.multiple_of(place * rows, 16), rows)
        copies.append(pltpu.make_async_copy(piece, features.at[here], sems.at[k]))
    for copy in copies:
        copy.start()
    for copy in copies:
        copy.wait()
    total = lax.dot_general(
        ranked[...], features[...], ROWS_BY_ROWS, preferred_element_type=jnp.float32
    )
    result[...] = (coefficient_of(owner, length, mine) * total).astype(result.dtype)
    columns = 4 * rows
    target = out.at[0, :, pl.ds(pl.multiple_of(chip * columns, 128), columns)]
    copy = pltpu.make_async_copy(result, target, sems.at[4])
    copy.start()
    copy.wait()


def on_chips(
    tokens,
    gate_weight,
    up_weight,
    down_weight,
    adapter_in,
    adapter_out,
    cotangent,
    block_owner,
    block_length,
    placement,
):
    f32, bf16 = jnp.float32, jnp.bfloat16
    me, core = lax.axis_index("batch").reshape(1), lax.axis_index("tensor").reshape(1)
    place = jnp.concatenate([me, core])
    mine = lax.dynamic_slice_in_dim(placement, lax.axis_index(("batch", "tensor")), 1)
    width = gate_weight.shape[1]
    model_width = gate_weight.shape[0]
    token_count, columns = cotangent.shape
    rank = adapter_in.shape[1]
    row_count = tokens.shape[0]

    def flip(piece, k):
        return lax.ppermute(piece, "batch", [(i, i ^ k) for i in range(8)])

    def to_other_core(piece):
        return lax.ppermute(piece, "tensor", [(0, 1), (1, 0)])

    def along_z(piece):
        return {0: piece, **{k: flip(piece, k) for k in (2, 4, 6)}}

    def then_along_y(line):
        return [line[k] if k in line else flip(line[k ^ 1], 1) for k in range(8)]

    own = then_along_y(along_z(tokens))
    other = [to_other_core(piece) for piece in own]
    cot_t = cotangent.T
    cot_and_back = kernel_call(
        back_body,
        jax.ShapeDtypeStruct((columns + rank, token_count), bf16),
        [IN_SMEM, IN_SMEM, IN_VMEM, IN_VMEM],
        flops=4 * rank * columns * token_count,
        moved=2 * adapter_out.size,
    )(block_owner, block_length, adapter_out, cot_t)
    rows = kernel_call(
        assemble_body,
        jax.ShapeDtypeStruct((token_count, model_width), bf16),
        [IN_SMEM, IN_SMEM] + [IN_VMEM] * 16,
        flops=0,
        moved=4 * token_count * model_width,
    )(me, core, *own, *other)
    line = along_z(cot_and_back)
    stack = jax.ShapeDtypeStruct((4, columns + rank, token_count), bf16)
    column = kernel_call(
        stack_body, stack, [IN_SMEM] + [IN_VMEM] * 4, flops=0, moved=0
    )(me, *[line[k] for k in (0, 2, 4, 6)])
    both = jax.ShapeDtypeStruct((8, columns + rank, token_count), bf16)
    gathered = kernel_call(
        interleave_body, both, [IN_SMEM] + [IN_VMEM] * 2, flops=0, moved=0
    )(me, column, flip(column, 1))
    gathered_other = to_other_core(gathered)

    gate_value = lax.dot_general(gate_weight.T, rows, ROWS_BY_ROWS, preferred_element_type=f32)
    up_value = lax.dot_general(up_weight.T, rows, ROWS_BY_ROWS, preferred_element_type=f32)
    hidden = (jax.nn.silu(gate_value) * up_value).astype(bf16)
    line = along_z(hidden)
    hidden_own = then_along_y(line)
    base_part = lax.dot_general(
        hidden, down_weight, (((0,), (0,)), ((), ())), preferred_element_type=f32
    ).astype(bf16)
    hidden_other = [to_other_core(piece) for piece in hidden_own]
    halves = jax.ShapeDtypeStruct((8 * columns + rank, token_count), bf16)
    kept, leaving = kernel_call(
        split_body,
        [halves, halves],
        [IN_SMEM, IN_SMEM] + [IN_VMEM] * 3,
        flops=4 * rank * width * token_count,
        moved=4 * token_count * model_width,
    )(block_owner, core, base_part, hidden, adapter_in)
    quarter = jax.ShapeDtypeStruct((4 * columns + rank, token_count), bf16)
    stays, leaving = kernel_call(
        add_body, [quarter, quarter], [IN_SMEM] + [IN_VMEM] * 2, flops=0, moved=0
    )(me, kept, to_other_core(leaving))
    share = jax.ShapeDtypeStruct((columns + rank, token_count), bf16)
    shares = kernel_call(
        add_pair_body, [share] * 4, [IN_SMEM] + [IN_VMEM] * 2 + [IN_HBM] * 3, flops=0, moved=0
    )(me, stays, flip(leaving, 1), *[line[k] for k in (2, 4, 6)])
    shares = [shares[0]] + [flip(shares[z], 2 * z) for z in (1, 2, 3)]
    mixed, low_chosen = kernel_call(
        final_body,
        [
            jax.ShapeDtypeStruct((columns, token_count), bf16),
            jax.ShapeDtypeStruct((rank, token_count), bf16),
        ],
        [IN_SMEM] * 3 + [IN_VMEM] * 5,
        flops=4 * rank * columns * token_count,
        moved=2 * halves.size,
    )(block_owner, block_length, mine, adapter_out, *shares)
    cot_all, back_chosen = kernel_call(
        gathered_body,
        [
            jax.ShapeDtypeStruct((model_width, token_count), bf16),
            jax.ShapeDtypeStruct((rank, token_count), bf16),
        ],
        [IN_SMEM] * 3 + [IN_VMEM] * 2,
        flops=0,
        moved=4 * token_count * model_width,
    )(block_owner, mine, core, gathered, gathered_other)
    grad_out = kernel_call(
        grad_of_array_body,
        jax.ShapeDtypeStruct((1, rank, model_width), bf16),
        [IN_SMEM] * 3 + [IN_VMEM] * 2,
        flops=2 * rank * token_count * model_width,
        moved=3 * token_count * model_width,
    )(block_owner, block_length, mine, low_chosen, cot_all)
    grad_in = None
    for k in (0, 2, 4, 6):
        pieces = [hidden_own[k], hidden_other[k], hidden_own[k ^ 1], hidden_other[k ^ 1]]
        buffers = [] if grad_in is None else [grad_in]
        grad_in = pl.pallas_call(
            functools.partial(grad_of_pieces_body, flips=k),
            out_shape=jax.ShapeDtypeStruct((1, rank, 16 * width), bf16),
            in_specs=[IN_SMEM] * 4 + [IN_VMEM] + [IN_HBM] * (4 + len(buffers)),
            out_specs=IN_HBM,
            scratch_shapes=[
                pltpu.VMEM((4 * width, token_count), bf16),
                pltpu.VMEM((rank, 4 * width), bf16),
                pltpu.SemaphoreType.DMA((5,)),
            ],
            input_output_aliases={9: 0} if buffers else {},
            compiler_params=pltpu.CompilerParams(vmem_limit_bytes=16 << 20),
            cost_estimate=pl.CostEstimate(
                flops=GRAD_FLOPS,
                bytes_accessed=3 * token_count * 4 * width,
                transcendentals=0,
            ),
        )(block_owner, block_length, mine, place, back_chosen, *pieces, *buffers)
    return mixed.T, grad_in, grad_out


def partner_shifts(count):
    return [[(i, i ^ k) for i in range(count)] for k in range(1, count)]


def gather_pieces(piece, axis):
    count = lax.axis_size(axis)
    if count & (count - 1) or count > 8:
        return lax.all_gather(piece, axis)
    me = lax.axis_index(axis)
    whole = jnp.zeros((count,) + piece.shape, piece.dtype)
    whole = lax.dynamic_update_index_in_dim(whole, piece, me, 0)
    for k, pairs in enumerate(partner_shifts(count), 1):
        arrived = lax.ppermute(piece, axis, pairs)
        whole = lax.dynamic_update_index_in_dim(whole, arrived, me ^ k, 0)
    return whole


def exchange_sum(pieces, axis):
    count = lax.axis_size(axis)
    if count & (count - 1) or count > 8:
        arrived = lax.all_to_all(pieces, axis, split_axis=0, concat_axis=0, tiled=True)
        return arrived.astype(jnp.float32).sum(0)
    me = lax.axis_index(axis)
    total = lax.dynamic_index_in_dim(pieces, me, 0, keepdims=False).astype(jnp.float32)
    for k, pairs in enumerate(partner_shifts(count), 1):
        leaving = lax.dynamic_index_in_dim(pieces, me ^ k, 0, keepdims=False)
        total = total + lax.ppermute(leaving, axis, pairs).astype(jnp.float32)
    return total


def pair_gather(piece):
    count = lax.axis_size("tensor")
    if count != 2:
        return lax.all_gather(piece, "tensor")
    other = lax.ppermute(piece, "tensor", [(0, 1), (1, 0)])
    mine_first = lax.axis_index("tensor") == 0
    return jnp.stack([jnp.where(mine_first, piece, other), jnp.where(mine_first, other, piece)])


def on_any_mesh(
    tokens,
    gate_weight,
    up_weight,
    down_weight,
    adapter_in,
    adapter_out,
    cotangent,
    block_owner,
    block_length,
    placement,
):
    f32, bf16 = jnp.float32, jnp.bfloat16
    batch_count, tensor_count = lax.axis_size("batch"), lax.axis_size("tensor")
    core = lax.axis_index("tensor")
    width = gate_weight.shape[1]
    model_width = gate_weight.shape[0]
    columns = cotangent.shape[1]
    token_count = cotangent.shape[0]
    block_count = block_owner.shape[0]
    block_size = token_count // block_count
    rank = adapter_in.shape[1]

    token_block = lax.broadcasted_iota(jnp.int32, (block_count, block_size), 0).reshape(-1)
    position = lax.broadcasted_iota(jnp.int32, (block_count, block_size), 1).reshape(-1)
    token_owner = jnp.repeat(block_owner, block_size)
    live = position < jnp.repeat(block_length, block_size)
    own_block = lax.broadcasted_iota(jnp.int32, (block_count, 1, 1), 0) == token_block

    def in_rank_space(matrices, features):
        every = jnp.dot(
            matrices.reshape(block_count * rank, -1), features, preferred_element_type=f32
        )
        return jnp.where(own_block, every.reshape(block_count, rank, token_count), 0.0).sum(0)

    in_blocks = adapter_in[block_owner]
    out_blocks = adapter_out[block_owner]
    cot_t = cotangent.T
    half = gather_pieces(tokens, "batch").reshape(token_count, -1)
    halves = pair_gather(half)
    rows = jnp.concatenate([halves[c] for c in range(tensor_count)], axis=1)

    back_part = jnp.where(live, in_rank_space(out_blocks, cot_t), 0.0).astype(bf16)
    cot_all = gather_pieces(cot_t, "batch")

    def weights_first(weight, values):
        return lax.dot_general(
            weight, values, (((0,), (1,)), ((), ())), preferred_element_type=f32
        )

    gate_value = weights_first(gate_weight, rows)
    up_value = weights_first(up_weight, rows)
    hidden = (jax.nn.silu(gate_value) * up_value).astype(bf16)
    hidden_all = gather_pieces(hidden, "batch")

    low_part = in_rank_space(in_blocks, hidden)
    base_part = lax.dot_general(
        down_weight, hidden, (((0,), (0,)), ((), ())), preferred_element_type=f32
    ).astype(bf16)
    base_part = base_part.reshape(batch_count, tensor_count, columns, token_count)
    ranked = jnp.concatenate([low_part.astype(bf16), back_part], axis=0)
    if tensor_count == 2:
        leaving = lax.dynamic_index_in_dim(base_part, 1 - core, 1, keepdims=False)
        kept = lax.dynamic_index_in_dim(base_part, core, 1, keepdims=False)
        arrived, ranked_other = lax.ppermute((leaving, ranked), "tensor", [(0, 1), (1, 0)])
        chip_base = (kept.astype(f32) + arrived.astype(f32)).astype(bf16)
        chip_ranked = (ranked.astype(f32) + ranked_other.astype(f32)).astype(bf16)
    else:
        chip_base = lax.psum_scatter(base_part, "tensor", scatter_dimension=1)
        chip_ranked = lax.psum(ranked, "tensor")
    leaving = jnp.concatenate(
        [chip_base, jnp.broadcast_to(chip_ranked, (batch_count,) + chip_ranked.shape)], axis=1
    )
    total = exchange_sum(leaving, "batch")
    base_sum = total[:columns]
    low = total[columns : columns + rank].astype(bf16)
    back = total[columns + rank :].astype(bf16)

    spread = jnp.where(own_block, low[None], jnp.zeros((), bf16)).reshape(-1, token_count)
    contribution = lax.dot_general(
        out_blocks.reshape(block_count * rank, columns),
        spread,
        (((0,), (0,)), ((), ())),
        preferred_element_type=f32,
    )
    mixed = (base_sum + lowrank_adapter_scale * contribution).astype(bf16).T

    slot = lax.axis_index(("batch", "tensor"))
    owner = placement[slot]
    count = jnp.where(block_owner == owner, block_length, 0).sum().astype(f32)
    coefficient = lowrank_adapter_scale / jnp.maximum(count, 1.0)
    chosen = token_owner == owner
    low_chosen = jnp.where(chosen & live, low, jnp.zeros((), bf16))
    back_chosen = jnp.where(chosen, back, jnp.zeros((), bf16))

    def slot_grad(ranked_values, pieces):
        both = pair_gather(pieces)
        features = jnp.swapaxes(both, 0, 1).reshape(-1, token_count)
        grad = lax.dot_general(
            ranked_values, features, (((1,), (1,)), ((), ())), preferred_element_type=f32
        )
        return (coefficient * grad).astype(bf16)[None]

    return mixed, slot_grad(back_chosen, hidden_all), slot_grad(low_chosen, cot_all)


def solution(mesh):
    placed = (
        P(("groups", "batch"), "tensor"),
        P(None, ("batch", "tensor")),
        P(None, ("batch", "tensor")),
        P(("batch", "tensor"), None),
        P("groups", None, ("batch", "tensor")),
        P("groups", None, ("batch", "tensor")),
        P("groups", ("batch", "tensor")),
        P("groups"),
        P("groups"),
        P("groups"),
    )
    on_device = on_any_mesh
    if mesh.shape["batch"] == 8 and mesh.shape["tensor"] == 2:
        on_device = on_chips
    return jax.shard_map(
        on_device,
        mesh=mesh,
        in_specs=placed,
        out_specs=(
            P("groups", ("batch", "tensor")),
            P(("groups", "batch", "tensor"), None, None),
            P(("groups", "batch", "tensor"), None, None),
        ),
        check_vma=False,
    )
```

```python
import functools

import jax
import jax.numpy as jnp
from jax import lax
from jax.experimental import pallas as pl
from jax.experimental.pallas import tpu as pltpu
from jax.sharding import PartitionSpec as P

lowrank_adapter_scale = 2.0

ROWS_BY_ROWS = (((1,), (1,)), ((), ()))
ASSEMBLE_FLOPS = 0
GRAD_FLOPS = 20000000000
FINAL_FLOPS = 20000000000
ADD_FLOPS = 0
PAIR_FLOPS = 0
SPLIT_FLOPS = 0
IN_VMEM = pl.BlockSpec(memory_space=pltpu.VMEM)
IN_HBM = pl.BlockSpec(memory_space=pl.ANY)
IN_SMEM = pl.BlockSpec(memory_space=pltpu.SMEM)


def kernel_call(
    body, out_shape, in_specs, scratch=(), out_specs=None, limit=16, aliases=None, flops=0
):
    return pl.pallas_call(
        body,
        out_shape=out_shape,
        in_specs=in_specs,
        out_specs=jax.tree.map(lambda _: IN_VMEM, out_shape) if out_specs is None else out_specs,
        scratch_shapes=list(scratch),
        input_output_aliases=aliases or {},
        compiler_params=pltpu.CompilerParams(vmem_limit_bytes=limit << 20),
        cost_estimate=pl.CostEstimate(flops=flops, bytes_accessed=0, transcendentals=0),
    )


class Facts:
    def __init__(self, ref):
        self.ref = ref
        self.blocks = (ref.shape[0] - 3) // 2
        self.batch, self.core, self.slot_owner = ref[0], ref[1], ref[2]

    def owner(self, block):
        return self.ref[3 + block]

    def length(self, block):
        return self.ref[3 + self.blocks + block]

    def lanes(self, token_count):
        lane = lax.broadcasted_iota(jnp.int32, (1, token_count), 1)
        size = token_count // self.blocks
        return lane, size, [(lane >= b * size) & (lane < (b + 1) * size) for b in range(self.blocks)]

    def live(self, token_count):
        lane, size, blocks = self.lanes(token_count)
        live = lane < 0
        for b in range(self.blocks):
            live = live | (blocks[b] & (lane < b * size + self.length(b)))
        return live

    def chosen(self, token_count):
        lane, _, blocks = self.lanes(token_count)
        chosen = lane < 0
        for b in range(self.blocks):
            mine = jnp.where(self.owner(b) == self.slot_owner, token_count, 0)
            chosen = chosen | (blocks[b] & (lane < mine))
        return chosen

    def coefficient(self):
        count = jnp.int32(0)
        for b in range(self.blocks):
            count = count + jnp.where(self.owner(b) == self.slot_owner, self.length(b), 0)
        return lowrank_adapter_scale / jnp.maximum(count, 1).astype(jnp.float32)


def prepare_body(owner, length, placement, adapter_out, adapter_in, cot, piece, *refs):
    facts, cot_and_back, out_blocks, in_blocks, passed, sems = refs
    passed[...] = piece[...]
    block_count = owner.shape[0]
    facts[0], facts[1] = lax.axis_index("batch"), lax.axis_index("tensor")
    facts[2] = placement[lax.axis_index("batch") * 2 + lax.axis_index("tensor")]
    for b in range(block_count):
        facts[3 + b] = owner[b]
        facts[3 + block_count + b] = length[b]
    facts = Facts(facts)
    copies = []
    for b in range(facts.blocks):
        for i, (source, target) in enumerate(((adapter_out, out_blocks), (adapter_in, in_blocks))):
            copies.append(
                pltpu.make_async_copy(source.at[facts.owner(b)], target.at[b], sems.at[i, b])
            )
    for copy in copies:
        copy.start()
    columns, token_count = cot.shape
    for b in range(cot_and_back.shape[0]):
        cot_and_back[b, :columns] = cot[...]
    for copy in copies:
        copy.wait()
    _, _, blocks = facts.lanes(token_count)
    total = jnp.zeros((out_blocks.shape[1], token_count), jnp.float32)
    for b in range(facts.blocks):
        every = jnp.dot(out_blocks[b], cot[...], preferred_element_type=jnp.float32)
        total = jnp.where(blocks[b], every, total)
    total = jnp.where(facts.live(token_count), total, 0.0)
    for b in range(cot_and_back.shape[0]):
        cot_and_back[b, columns:] = total.astype(cot_and_back.dtype)


def run_copies(pairs, sems):
    copies = [
        pltpu.make_async_copy(source, target, sems.at[i])
        for i, (source, target) in enumerate(pairs)
    ]
    for copy in copies:
        copy.start()
    for copy in copies:
        copy.wait()


def assemble_body(facts, *refs):
    facts, pieces, out = Facts(facts), refs[:-1], refs[-1]
    count = len(pieces) // 2
    rows, half = pieces[0].shape
    for i, piece in enumerate(pieces):
        row = pl.multiple_of((facts.batch ^ (i % count)) * rows, rows)
        core = facts.core if i < count else 1 - facts.core
        out[pl.ds(row, rows), pl.ds(pl.multiple_of(core * half, 128), half)] = piece[...]


def split_body(facts, base, hidden, in_blocks, *refs):
    facts, kept, leaving = Facts(facts), refs[-2], refs[-1]
    token_count = base.shape[0]
    rank = in_blocks.shape[1]
    columns = (kept.shape[0] - rank) // 8
    for b in range(8):
        both = base[:, b * 2 * columns : (b + 1) * 2 * columns].astype(jnp.float32).T
        both = both.astype(kept.dtype)
        here = pl.ds(b * columns, columns)

        @pl.when(facts.core == 0)
        def _():
            kept[here] = both[:columns]
            leaving[here] = both[columns:]

        @pl.when(facts.core != 0)
        def _():
            kept[here] = both[columns:]
            leaving[here] = both[:columns]

    _, _, blocks = facts.lanes(token_count)
    low = jnp.zeros((rank, token_count), jnp.float32)
    for b in range(facts.blocks):
        every = jnp.dot(in_blocks[b], hidden[...], preferred_element_type=jnp.float32)
        low = jnp.where(blocks[b], every, low)
    tail = pl.ds(8 * columns, rank)
    kept[tail] = low.astype(kept.dtype)
    leaving[tail] = low.astype(kept.dtype)


def add_body(facts, kept, arrived, own, leaving):
    rank = own.shape[0] - (kept.shape[0] - own.shape[0])
    columns = (own.shape[0] - rank) // 4
    side = Facts(facts).batch % 2

    def added(first, count):
        here = pl.ds(first, count)
        total = kept[here].astype(jnp.float32) + arrived[here].astype(jnp.float32)
        return total.astype(own.dtype)

    for z in range(4):
        here = pl.ds(z * columns, columns)
        own[here] = added(pl.multiple_of((2 * z + side) * columns, 16), columns)
        leaving[here] = added(pl.multiple_of((2 * z + 1 - side) * columns, 16), columns)
    low = added(8 * columns, rank)
    own[4 * columns :] = low
    leaving[4 * columns :] = low


def add_pair_body(facts, own, arrived, *refs):
    outs = refs[-4:]
    columns = (own.shape[0] - outs[0].shape[0]) // 3
    place = Facts(facts).batch // 2

    def added(first, count):
        here = pl.ds(first, count)
        total = own[here].astype(jnp.float32) + arrived[here].astype(jnp.float32)
        return total.astype(own.dtype)

    low = added(4 * columns, own.shape[0] - 4 * columns)
    for flip, out in enumerate(outs):
        out[:columns] = added(pl.multiple_of((place ^ flip) * columns, 16), columns)
        out[columns:] = low


def final_body(facts, out_blocks, gathered, gathered_other, *refs):
    facts, arrived, (mixed, grad, ranked, features) = Facts(facts), refs[:-4], refs[-4:]
    columns, token_count = mixed.shape
    total = arrived[0][...].astype(jnp.float32)
    for share in arrived[1:]:
        total = total + share[...].astype(jnp.float32)
    low = total[columns:]
    _, _, blocks = facts.lanes(token_count)
    contribution = jnp.zeros(mixed.shape, jnp.float32)
    for b in range(facts.blocks):
        every = lax.dot_general(
            out_blocks[b],
            low.astype(jnp.bfloat16),
            (((0,), (0,)), ((), ())),
            preferred_element_type=jnp.float32,
        )
        contribution = jnp.where(blocks[b], every, contribution)
    mixed[...] = (total[:columns] + lowrank_adapter_scale * contribution).astype(mixed.dtype)
    chosen = facts.chosen(token_count) & facts.live(token_count)
    ranked[...] = jnp.where(chosen, low, 0.0).astype(ranked.dtype)
    for half, pieces in ((facts.core, gathered), (1 - facts.core, gathered_other)):
        for b in range(pieces.shape[0]):
            here = pl.ds(pl.multiple_of((2 * b + half) * columns, 16), columns)
            features[here] = pieces[b, :columns]
    total = lax.dot_general(
        ranked[...], features[...], ROWS_BY_ROWS, preferred_element_type=jnp.float32
    )
    grad[0] = (facts.coefficient() * total).astype(grad.dtype)


def pass_body(*refs):
    pass


def back_body(facts, gathered, gathered_other, ranked):
    back = jnp.zeros(ranked.shape, jnp.float32)
    first = gathered.shape[1] - ranked.shape[0]
    for pieces in (gathered, gathered_other):
        for b in range(pieces.shape[0]):
            back = back + pieces[b, first:].astype(jnp.float32)
    chosen = Facts(facts).chosen(ranked.shape[1])
    ranked[...] = jnp.where(chosen, back, 0.0).astype(ranked.dtype)


def in_grad_body(facts, ranked, *refs, flips):
    pieces, (out, features, result, sems) = refs[:8], refs[-4:]
    facts = Facts(facts)
    rows = pieces[0].shape[0]
    side = facts.batch % 2
    factor = facts.coefficient()
    leaving = []
    for i, flip in enumerate(flips):
        for j in range(4):
            y = side if j < 2 else 1 - side
            core = facts.core if j % 2 == 0 else 1 - facts.core
            here = pl.ds(pl.multiple_of((y * 2 + core) * rows, 16), rows)
            features[i, here] = pieces[4 * i + j][...]
        total = lax.dot_general(
            ranked[...], features[i], ROWS_BY_ROWS, preferred_element_type=jnp.float32
        )
        result[i] = (factor * total).astype(result.dtype)
        columns = 4 * rows
        first = ((facts.batch ^ flip) // 2) * columns
        target = out.at[0, :, pl.ds(pl.multiple_of(first, 128), columns)]
        leaving.append(pltpu.make_async_copy(result.at[i], target, sems.at[i]))
        leaving[-1].start()
    for copy in leaving:
        copy.wait()


def on_chips(
    tokens,
    gate_weight,
    up_weight,
    down_weight,
    adapter_in,
    adapter_out,
    cotangent,
    block_owner,
    block_length,
    placement,
):
    f32, bf16 = jnp.float32, jnp.bfloat16
    width = gate_weight.shape[1]
    model_width = gate_weight.shape[0]
    token_count, columns = cotangent.shape
    rank = adapter_in.shape[1]
    block_count = block_owner.shape[0]
    def array(*shape):
        return jax.ShapeDtypeStruct(shape, bf16)

    def flip(piece, k):
        return lax.ppermute(piece, "batch", [(i, i ^ k) for i in range(8)])

    def to_other_core(piece):
        return lax.ppermute(piece, "tensor", [(0, 1), (1, 0)])

    def along_z(piece):
        return {0: piece, **{k: flip(piece, k) for k in (2, 4, 6)}}

    def then_along_y(line):
        return [line[k] if k in line else flip(line[k ^ 1], 1) for k in range(8)]

    line = along_z(tokens)
    facts, cot_and_back, out_blocks, in_blocks, line[2] = kernel_call(
        prepare_body,
        [
            jax.ShapeDtypeStruct((3 + 2 * block_count,), jnp.int32),
            array(8, columns + rank, token_count),
            array(block_count, rank, columns),
            array(block_count, rank, width),
            array(*tokens.shape),
        ],
        [IN_SMEM] * 3 + [IN_HBM, IN_HBM, IN_VMEM, IN_VMEM],
        out_specs=[IN_SMEM] + [IN_VMEM] * 4,
        scratch=[pltpu.SemaphoreType.DMA((2, block_count))],
        limit=56,
    )(block_owner, block_length, placement, adapter_out, adapter_in, cotangent.T, line[2])
    own = then_along_y(line)
    other = [to_other_core(piece) for piece in own]
    gathered = lax.all_to_all(
        cot_and_back, "batch", split_axis=0, concat_axis=0, tiled=True
    )
    rows = kernel_call(
        assemble_body,
        array(token_count, model_width),
        [IN_SMEM] + [IN_VMEM] * 16,
        flops=ASSEMBLE_FLOPS,
    )(facts, *own, *other)
    gate_value = lax.dot_general(gate_weight.T, rows, ROWS_BY_ROWS, preferred_element_type=f32)
    up_value = lax.dot_general(up_weight.T, rows, ROWS_BY_ROWS, preferred_element_type=f32)
    hidden = (jax.nn.silu(gate_value) * up_value).astype(bf16)
    base_part = lax.dot_general(
        hidden, down_weight, (((0,), (0,)), ((), ())), preferred_element_type=f32
    ).astype(bf16)
    kept, leaving = kernel_call(
        split_body,
        [array(8 * columns + rank, token_count)] * 2,
        [IN_SMEM] + [IN_VMEM] * 3,
        flops=SPLIT_FLOPS,
    )(facts, base_part, hidden, in_blocks)
    stays, leaving = kernel_call(
        add_body,
        [array(4 * columns + rank, token_count)] * 2,
        [IN_SMEM] + [IN_VMEM] * 2,
        flops=ADD_FLOPS,
    )(facts, kept, to_other_core(leaving))
    line = along_z(hidden)
    gathered = kernel_call(
        pass_body,
        array(8, columns + rank, token_count),
        [IN_HBM] * 2,
        out_specs=IN_HBM,
        aliases={0: 0},
    )(gathered, stays)
    gathered_other = to_other_core(gathered)
    hidden_own = then_along_y(line)
    hidden_other = [to_other_core(piece) for piece in hidden_own]
    shares = kernel_call(
        add_pair_body,
        [array(columns + rank, token_count)] * 4,
        [IN_SMEM] + [IN_VMEM] * 2 + [IN_HBM] * 3,
        flops=PAIR_FLOPS,
    )(facts, stays, flip(leaving, 1), *[line[k] for k in (2, 4, 6)])
    shares = [shares[0]] + [flip(shares[z], 2 * z) for z in (1, 2, 3)]
    mixed, grad_out, low_chosen = kernel_call(
        final_body,
        [array(columns, token_count), array(1, rank, model_width), array(rank, token_count)],
        [IN_SMEM] + [IN_VMEM] * 7,
        scratch=[pltpu.VMEM((model_width, token_count), bf16)],
        flops=FINAL_FLOPS,
    )(facts, out_blocks, gathered, gathered_other, *shares)
    back_chosen = kernel_call(back_body, array(rank, token_count), [IN_SMEM] + [IN_VMEM] * 2)(
        facts, gathered, gathered_other
    )
    grad_in = None
    for flips in ((0, 2), (4, 6)):
        order = [p for k in flips for p in (k, k ^ 1)]
        pieces = [p for k in order for p in (hidden_own[k], hidden_other[k])]
        if grad_in is None:
            last, aliases = [], {}
        else:
            last, aliases = [grad_in, low_chosen], {10: 0}
        grad_in = kernel_call(
            functools.partial(in_grad_body, flips=flips),
            array(1, rank, 16 * width),
            [IN_SMEM] + [IN_VMEM] * 9 + [IN_HBM] * len(last),
            scratch=[
                pltpu.VMEM((2, 4 * width, token_count), bf16),
                pltpu.VMEM((2, rank, 4 * width), bf16),
                pltpu.SemaphoreType.DMA((2,)),
            ],
            out_specs=IN_HBM,
            aliases=aliases,
            flops=GRAD_FLOPS,
        )(facts, back_chosen, *pieces, *last)
    return mixed.T, grad_in, grad_out


def partner_shifts(count):
    return [[(i, i ^ k) for i in range(count)] for k in range(1, count)]


def gather_pieces(piece, axis):
    count = lax.axis_size(axis)
    if count & (count - 1) or count > 8:
        return lax.all_gather(piece, axis)
    me = lax.axis_index(axis)
    whole = jnp.zeros((count,) + piece.shape, piece.dtype)
    whole = lax.dynamic_update_index_in_dim(whole, piece, me, 0)
    for k, pairs in enumerate(partner_shifts(count), 1):
        arrived = lax.ppermute(piece, axis, pairs)
        whole = lax.dynamic_update_index_in_dim(whole, arrived, me ^ k, 0)
    return whole


def exchange_sum(pieces, axis):
    count = lax.axis_size(axis)
    if count & (count - 1) or count > 8:
        arrived = lax.all_to_all(pieces, axis, split_axis=0, concat_axis=0, tiled=True)
        return arrived.astype(jnp.float32).sum(0)
    me = lax.axis_index(axis)
    total = lax.dynamic_index_in_dim(pieces, me, 0, keepdims=False).astype(jnp.float32)
    for k, pairs in enumerate(partner_shifts(count), 1):
        leaving = lax.dynamic_index_in_dim(pieces, me ^ k, 0, keepdims=False)
        total = total + lax.ppermute(leaving, axis, pairs).astype(jnp.float32)
    return total


def pair_gather(piece):
    count = lax.axis_size("tensor")
    if count != 2:
        return lax.all_gather(piece, "tensor")
    other = lax.ppermute(piece, "tensor", [(0, 1), (1, 0)])
    mine_first = lax.axis_index("tensor") == 0
    return jnp.stack([jnp.where(mine_first, piece, other), jnp.where(mine_first, other, piece)])


def on_any_mesh(
    tokens,
    gate_weight,
    up_weight,
    down_weight,
    adapter_in,
    adapter_out,
    cotangent,
    block_owner,
    block_length,
    placement,
):
    f32, bf16 = jnp.float32, jnp.bfloat16
    batch_count, tensor_count = lax.axis_size("batch"), lax.axis_size("tensor")
    core = lax.axis_index("tensor")
    width = gate_weight.shape[1]
    model_width = gate_weight.shape[0]
    columns = cotangent.shape[1]
    token_count = cotangent.shape[0]
    block_count = block_owner.shape[0]
    block_size = token_count // block_count
    rank = adapter_in.shape[1]

    token_block = lax.broadcasted_iota(jnp.int32, (block_count, block_size), 0).reshape(-1)
    position = lax.broadcasted_iota(jnp.int32, (block_count, block_size), 1).reshape(-1)
    token_owner = jnp.repeat(block_owner, block_size)
    live = position < jnp.repeat(block_length, block_size)
    own_block = lax.broadcasted_iota(jnp.int32, (block_count, 1, 1), 0) == token_block

    def in_rank_space(matrices, features):
        every = jnp.dot(
            matrices.reshape(block_count * rank, -1), features, preferred_element_type=f32
        )
        return jnp.where(own_block, every.reshape(block_count, rank, token_count), 0.0).sum(0)

    in_blocks = adapter_in[block_owner]
    out_blocks = adapter_out[block_owner]
    cot_t = cotangent.T
    half = gather_pieces(tokens, "batch").reshape(token_count, -1)
    halves = pair_gather(half)
    rows = jnp.concatenate([halves[c] for c in range(tensor_count)], axis=1)

    back_part = jnp.where(live, in_rank_space(out_blocks, cot_t), 0.0).astype(bf16)
    cot_all = gather_pieces(cot_t, "batch")

    def weights_first(weight, values):
        return lax.dot_general(
            weight, values, (((0,), (1,)), ((), ())), preferred_element_type=f32
        )

    gate_value = weights_first(gate_weight, rows)
    up_value = weights_first(up_weight, rows)
    hidden = (jax.nn.silu(gate_value) * up_value).astype(bf16)
    hidden_all = gather_pieces(hidden, "batch")

    low_part = in_rank_space(in_blocks, hidden)
    base_part = lax.dot_general(
        down_weight, hidden, (((0,), (0,)), ((), ())), preferred_element_type=f32
    ).astype(bf16)
    base_part = base_part.reshape(batch_count, tensor_count, columns, token_count)
    ranked = jnp.concatenate([low_part.astype(bf16), back_part], axis=0)
    if tensor_count == 2:
        leaving = lax.dynamic_index_in_dim(base_part, 1 - core, 1, keepdims=False)
        kept = lax.dynamic_index_in_dim(base_part, core, 1, keepdims=False)
        arrived, ranked_other = lax.ppermute((leaving, ranked), "tensor", [(0, 1), (1, 0)])
        chip_base = (kept.astype(f32) + arrived.astype(f32)).astype(bf16)
        chip_ranked = (ranked.astype(f32) + ranked_other.astype(f32)).astype(bf16)
    else:
        chip_base = lax.psum_scatter(base_part, "tensor", scatter_dimension=1)
        chip_ranked = lax.psum(ranked, "tensor")
    leaving = jnp.concatenate(
        [chip_base, jnp.broadcast_to(chip_ranked, (batch_count,) + chip_ranked.shape)], axis=1
    )
    total = exchange_sum(leaving, "batch")
    base_sum = total[:columns]
    low = total[columns : columns + rank].astype(bf16)
    back = total[columns + rank :].astype(bf16)

    spread = jnp.where(own_block, low[None], jnp.zeros((), bf16)).reshape(-1, token_count)
    contribution = lax.dot_general(
        out_blocks.reshape(block_count * rank, columns),
        spread,
        (((0,), (0,)), ((), ())),
        preferred_element_type=f32,
    )
    mixed = (base_sum + lowrank_adapter_scale * contribution).astype(bf16).T

    slot = lax.axis_index(("batch", "tensor"))
    owner = placement[slot]
    count = jnp.where(block_owner == owner, block_length, 0).sum().astype(f32)
    coefficient = lowrank_adapter_scale / jnp.maximum(count, 1.0)
    chosen = token_owner == owner
    low_chosen = jnp.where(chosen & live, low, jnp.zeros((), bf16))
    back_chosen = jnp.where(chosen, back, jnp.zeros((), bf16))

    def slot_grad(ranked_values, pieces):
        both = pair_gather(pieces)
        features = jnp.swapaxes(both, 0, 1).reshape(-1, token_count)
        grad = lax.dot_general(
            ranked_values, features, (((1,), (1,)), ((), ())), preferred_element_type=f32
        )
        return (coefficient * grad).astype(bf16)[None]

    return mixed, slot_grad(back_chosen, hidden_all), slot_grad(low_chosen, cot_all)


def solution(mesh):
    placed = (
        P(("groups", "batch"), "tensor"),
        P(None, ("batch", "tensor")),
        P(None, ("batch", "tensor")),
        P(("batch", "tensor"), None),
        P("groups", None, ("batch", "tensor")),
        P("groups", None, ("batch", "tensor")),
        P("groups", ("batch", "tensor")),
        P("groups"),
        P("groups"),
        P("groups"),
    )
    on_device = on_any_mesh
    if mesh.shape["batch"] == 8 and mesh.shape["tensor"] == 2:
        on_device = on_chips
    return jax.shard_map(
        on_device,
        mesh=mesh,
        in_specs=placed,
        out_specs=(
            P("groups", ("batch", "tensor")),
            P(("groups", "batch", "tensor"), None, None),
            P(("groups", "batch", "tensor"), None, None),
        ),
        check_vma=False,
    )
```

```python
import functools

import jax
import jax.numpy as jnp
from jax import lax
from jax.experimental import pallas as pl
from jax.experimental.pallas import tpu as pltpu
from jax.sharding import PartitionSpec as P

lowrank_adapter_scale = 2.0

ROWS_BY_ROWS = (((1,), (1,)), ((), ()))
ASSEMBLE_FLOPS = 0
GRAD_FLOPS = 20000000000
FINAL_FLOPS = 8000000000
ADD_FLOPS = 0
PAIR_FLOPS = 0
SPLIT_FLOPS = 0
IN_VMEM = pl.BlockSpec(memory_space=pltpu.VMEM)
IN_HBM = pl.BlockSpec(memory_space=pl.ANY)
IN_SMEM = pl.BlockSpec(memory_space=pltpu.SMEM)


def kernel_call(
    body, out_shape, in_specs, scratch=(), out_specs=None, limit=16, aliases=None, flops=0
):
    return pl.pallas_call(
        body,
        out_shape=out_shape,
        in_specs=in_specs,
        out_specs=jax.tree.map(lambda _: IN_VMEM, out_shape) if out_specs is None else out_specs,
        scratch_shapes=list(scratch),
        input_output_aliases=aliases or {},
        compiler_params=pltpu.CompilerParams(vmem_limit_bytes=limit << 20),
        cost_estimate=pl.CostEstimate(flops=flops, bytes_accessed=0, transcendentals=0),
    )


class Facts:
    def __init__(self, ref):
        self.ref = ref
        self.blocks = (ref.shape[0] - 3) // 2
        self.batch, self.core, self.slot_owner = ref[0], ref[1], ref[2]

    def owner(self, block):
        return self.ref[3 + block]

    def length(self, block):
        return self.ref[3 + self.blocks + block]

    def lanes(self, token_count):
        lane = lax.broadcasted_iota(jnp.int32, (1, token_count), 1)
        size = token_count // self.blocks
        return lane, size, [(lane >= b * size) & (lane < (b + 1) * size) for b in range(self.blocks)]

    def live(self, token_count):
        lane, size, blocks = self.lanes(token_count)
        live = lane < 0
        for b in range(self.blocks):
            live = live | (blocks[b] & (lane < b * size + self.length(b)))
        return live

    def chosen(self, token_count):
        lane, _, blocks = self.lanes(token_count)
        chosen = lane < 0
        for b in range(self.blocks):
            mine = jnp.where(self.owner(b) == self.slot_owner, token_count, 0)
            chosen = chosen | (blocks[b] & (lane < mine))
        return chosen

    def coefficient(self):
        count = jnp.int32(0)
        for b in range(self.blocks):
            count = count + jnp.where(self.owner(b) == self.slot_owner, self.length(b), 0)
        return lowrank_adapter_scale / jnp.maximum(count, 1).astype(jnp.float32)


def prepare_body(owner, length, placement, adapter_out, adapter_in, cot, piece, *refs):
    facts, cot_and_back, out_blocks, in_blocks, passed, sems = refs
    passed[...] = piece[...]
    block_count = owner.shape[0]
    facts[0], facts[1] = lax.axis_index("batch"), lax.axis_index("tensor")
    facts[2] = placement[lax.axis_index("batch") * 2 + lax.axis_index("tensor")]
    for b in range(block_count):
        facts[3 + b] = owner[b]
        facts[3 + block_count + b] = length[b]
    facts = Facts(facts)
    copies = []
    for b in range(facts.blocks):
        for i, (source, target) in enumerate(((adapter_out, out_blocks), (adapter_in, in_blocks))):
            copies.append(
                pltpu.make_async_copy(source.at[facts.owner(b)], target.at[b], sems.at[i, b])
            )
    for copy in copies:
        copy.start()
    columns, token_count = cot.shape
    for b in range(cot_and_back.shape[0]):
        cot_and_back[b, :columns] = cot[...]
    for copy in copies:
        copy.wait()
    _, _, blocks = facts.lanes(token_count)
    total = jnp.zeros((out_blocks.shape[1], token_count), jnp.float32)
    for b in range(facts.blocks):
        every = jnp.dot(out_blocks[b], cot[...], preferred_element_type=jnp.float32)
        total = jnp.where(blocks[b], every, total)
    total = jnp.where(facts.live(token_count), total, 0.0)
    for b in range(cot_and_back.shape[0]):
        cot_and_back[b, columns:] = total.astype(cot_and_back.dtype)


def run_copies(pairs, sems):
    copies = [
        pltpu.make_async_copy(source, target, sems.at[i])
        for i, (source, target) in enumerate(pairs)
    ]
    for copy in copies:
        copy.start()
    for copy in copies:
        copy.wait()


def assemble_body(*refs):
    pieces, out = refs[:-1], refs[-1]
    batch, own_core = lax.axis_index("batch"), lax.axis_index("tensor")
    count = len(pieces) // 2
    rows, half = pieces[0].shape
    for i, piece in enumerate(pieces):
        row = pl.multiple_of((batch ^ (i % count)) * rows, rows)
        core = own_core if i < count else 1 - own_core
        out[pl.ds(row, rows), pl.ds(pl.multiple_of(core * half, 128), half)] = piece[...]


def split_body(facts, base, hidden, in_blocks, *refs):
    facts, kept, leaving = Facts(facts), refs[-2], refs[-1]
    token_count = base.shape[0]
    rank = in_blocks.shape[1]
    columns = (kept.shape[0] - rank) // 8
    for b in range(8):
        both = base[:, b * 2 * columns : (b + 1) * 2 * columns].astype(jnp.float32).T
        both = both.astype(kept.dtype)
        here = pl.ds(b * columns, columns)

        @pl.when(facts.core == 0)
        def _():
            kept[here] = both[:columns]
            leaving[here] = both[columns:]

        @pl.when(facts.core != 0)
        def _():
            kept[here] = both[columns:]
            leaving[here] = both[:columns]

    _, _, blocks = facts.lanes(token_count)
    low = jnp.zeros((rank, token_count), jnp.float32)
    for b in range(facts.blocks):
        every = jnp.dot(in_blocks[b], hidden[...], preferred_element_type=jnp.float32)
        low = jnp.where(blocks[b], every, low)
    tail = pl.ds(8 * columns, rank)
    kept[tail] = low.astype(kept.dtype)
    leaving[tail] = low.astype(kept.dtype)


def add_body(facts, kept, arrived, own, leaving):
    rank = own.shape[0] - (kept.shape[0] - own.shape[0])
    columns = (own.shape[0] - rank) // 4
    side = Facts(facts).batch % 2

    def added(first, count):
        here = pl.ds(first, count)
        total = kept[here].astype(jnp.float32) + arrived[here].astype(jnp.float32)
        return total.astype(own.dtype)

    for z in range(4):
        here = pl.ds(z * columns, columns)
        own[here] = added(pl.multiple_of((2 * z + side) * columns, 16), columns)
        leaving[here] = added(pl.multiple_of((2 * z + 1 - side) * columns, 16), columns)
    low = added(8 * columns, rank)
    own[4 * columns :] = low
    leaving[4 * columns :] = low


def add_pair_body(facts, own, arrived, *refs):
    outs = refs[-4:]
    columns = (own.shape[0] - outs[0].shape[0]) // 3
    place = Facts(facts).batch // 2

    def added(first, count):
        here = pl.ds(first, count)
        total = own[here].astype(jnp.float32) + arrived[here].astype(jnp.float32)
        return total.astype(own.dtype)

    low = added(4 * columns, own.shape[0] - 4 * columns)
    for flip, out in enumerate(outs):
        out[:columns] = added(pl.multiple_of((place ^ flip) * columns, 16), columns)
        out[columns:] = low


def final_body(facts, out_blocks, gathered, gathered_other, *refs):
    facts, arrived, (mixed, grad, ranked, features) = Facts(facts), refs[:-4], refs[-4:]
    columns, token_count = mixed.shape
    total = arrived[0][...].astype(jnp.float32)
    for share in arrived[1:]:
        total = total + share[...].astype(jnp.float32)
    low = total[columns:]
    _, _, blocks = facts.lanes(token_count)
    contribution = jnp.zeros(mixed.shape, jnp.float32)
    for b in range(facts.blocks):
        every = lax.dot_general(
            out_blocks[b],
            low.astype(jnp.bfloat16),
            (((0,), (0,)), ((), ())),
            preferred_element_type=jnp.float32,
        )
        contribution = jnp.where(blocks[b], every, contribution)
    mixed[...] = (total[:columns] + lowrank_adapter_scale * contribution).astype(mixed.dtype)
    chosen = facts.chosen(token_count) & facts.live(token_count)
    ranked[...] = jnp.where(chosen, low, 0.0).astype(ranked.dtype)
    for half, pieces in ((facts.core, gathered), (1 - facts.core, gathered_other)):
        for b in range(pieces.shape[0]):
            here = pl.ds(pl.multiple_of((2 * b + half) * columns, 16), columns)
            features[here] = pieces[b, :columns]
    total = lax.dot_general(
        ranked[...], features[...], ROWS_BY_ROWS, preferred_element_type=jnp.float32
    )
    grad[0] = (facts.coefficient() * total).astype(grad.dtype)


def copy_body(source, _, target):
    target[...] = source[...]


def pass_body(*refs):
    pass


def back_body(facts, gathered, gathered_other, ranked):
    back = jnp.zeros(ranked.shape, jnp.float32)
    first = gathered.shape[1] - ranked.shape[0]
    for pieces in (gathered, gathered_other):
        for b in range(pieces.shape[0]):
            back = back + pieces[b, first:].astype(jnp.float32)
    chosen = Facts(facts).chosen(ranked.shape[1])
    ranked[...] = jnp.where(chosen, back, 0.0).astype(ranked.dtype)


def in_grad_body(facts, ranked, *refs, flips):
    pieces, (out, features, result, sems) = refs[:8], refs[-4:]
    facts = Facts(facts)
    rows = pieces[0].shape[0]
    side = facts.batch % 2
    factor = facts.coefficient()
    leaving = []
    for i, flip in enumerate(flips):
        for j in range(4):
            y = side if j < 2 else 1 - side
            core = facts.core if j % 2 == 0 else 1 - facts.core
            here = pl.ds(pl.multiple_of((y * 2 + core) * rows, 16), rows)
            features[i, here] = pieces[4 * i + j][...]
        total = lax.dot_general(
            ranked[...], features[i], ROWS_BY_ROWS, preferred_element_type=jnp.float32
        )
        result[i] = (factor * total).astype(result.dtype)
        columns = 4 * rows
        first = ((facts.batch ^ flip) // 2) * columns
        target = out.at[0, :, pl.ds(pl.multiple_of(first, 128), columns)]
        leaving.append(pltpu.make_async_copy(result.at[i], target, sems.at[i]))
        leaving[-1].start()
    for copy in leaving:
        copy.wait()


def on_chips(
    tokens,
    gate_weight,
    up_weight,
    down_weight,
    adapter_in,
    adapter_out,
    cotangent,
    block_owner,
    block_length,
    placement,
):
    f32, bf16 = jnp.float32, jnp.bfloat16
    width = gate_weight.shape[1]
    model_width = gate_weight.shape[0]
    token_count, columns = cotangent.shape
    rank = adapter_in.shape[1]
    block_count = block_owner.shape[0]
    def array(*shape):
        return jax.ShapeDtypeStruct(shape, bf16)

    def flip(piece, k):
        return lax.ppermute(piece, "batch", [(i, i ^ k) for i in range(8)])

    def to_other_core(piece):
        return lax.ppermute(piece, "tensor", [(0, 1), (1, 0)])

    def along_z(piece):
        return {0: piece, **{k: flip(piece, k) for k in (2, 4, 6)}}

    def then_along_y(line):
        return [line[k] if k in line else flip(line[k ^ 1], 1) for k in range(8)]

    line = along_z(tokens)
    arrived = line[2]
    facts, cot_and_back, out_blocks, in_blocks, line[2] = kernel_call(
        prepare_body,
        [
            jax.ShapeDtypeStruct((3 + 2 * block_count,), jnp.int32),
            array(8, columns + rank, token_count),
            array(block_count, rank, columns),
            array(block_count, rank, width),
            array(*tokens.shape),
        ],
        [IN_SMEM] * 3 + [IN_HBM, IN_HBM, IN_VMEM, IN_VMEM],
        out_specs=[IN_SMEM] + [IN_VMEM] * 4,
        scratch=[pltpu.SemaphoreType.DMA((2, block_count))],
        limit=56,
    )(block_owner, block_length, placement, adapter_out, adapter_in, cotangent.T, line[2])
    own = then_along_y(line)
    other = [to_other_core(piece) for piece in own]
    gathered = lax.all_to_all(
        cot_and_back, "batch", split_axis=0, concat_axis=0, tiled=True
    )
    rows = kernel_call(
        assemble_body,
        array(token_count, model_width),
        [IN_VMEM] * 16,
        flops=ASSEMBLE_FLOPS,
    )(*own[:2], arrived, *own[3:], *other)
    gate_value = lax.dot_general(gate_weight.T, rows, ROWS_BY_ROWS, preferred_element_type=f32)
    up_value = lax.dot_general(up_weight.T, rows, ROWS_BY_ROWS, preferred_element_type=f32)
    hidden = (jax.nn.silu(gate_value) * up_value).astype(bf16)
    base_part = lax.dot_general(
        hidden, down_weight, (((0,), (0,)), ((), ())), preferred_element_type=f32
    ).astype(bf16)
    kept, leaving = kernel_call(
        split_body,
        [array(8 * columns + rank, token_count)] * 2,
        [IN_SMEM] + [IN_VMEM] * 3,
        flops=SPLIT_FLOPS,
    )(facts, base_part, hidden, in_blocks)
    stays, leaving = kernel_call(
        add_body,
        [array(4 * columns + rank, token_count)] * 2,
        [IN_SMEM] + [IN_VMEM] * 2,
        flops=ADD_FLOPS,
    )(facts, kept, to_other_core(leaving))
    line = along_z(hidden)
    line[0] = kernel_call(copy_body, array(width, token_count), [IN_VMEM, IN_HBM])(
        hidden, line[2]
    )
    gathered = kernel_call(
        pass_body,
        array(8, columns + rank, token_count),
        [IN_HBM] * 2,
        out_specs=IN_HBM,
        aliases={0: 0},
    )(gathered, stays)
    gathered_other = to_other_core(gathered)
    hidden_own = then_along_y(line)
    hidden_other = [to_other_core(piece) for piece in hidden_own]
    shares = kernel_call(
        add_pair_body,
        [array(columns + rank, token_count)] * 4,
        [IN_SMEM] + [IN_VMEM] * 2 + [IN_HBM] * 3,
        flops=PAIR_FLOPS,
    )(facts, stays, flip(leaving, 1), line[2], line[2], line[2])
    shares = [shares[0]] + [flip(shares[z], 2 * z) for z in (1, 2, 3)]
    mixed, grad_out, low_chosen = kernel_call(
        final_body,
        [array(columns, token_count), array(1, rank, model_width), array(rank, token_count)],
        [IN_SMEM] + [IN_VMEM] * 7,
        scratch=[pltpu.VMEM((model_width, token_count), bf16)],
        flops=FINAL_FLOPS,
    )(facts, out_blocks, gathered, gathered_other, *shares)
    back_chosen = kernel_call(back_body, array(rank, token_count), [IN_SMEM] + [IN_VMEM] * 2)(
        facts, gathered, gathered_other
    )
    grad_in = None
    for flips in ((0, 2), (4, 6)):
        order = [p for k in flips for p in (k, k ^ 1)]
        pieces = [p for k in order for p in (hidden_own[k], hidden_other[k])]
        if grad_in is None:
            last, aliases = [], {}
        else:
            last, aliases = [grad_in, low_chosen], {10: 0}
        grad_in = kernel_call(
            functools.partial(in_grad_body, flips=flips),
            array(1, rank, 16 * width),
            [IN_SMEM] + [IN_VMEM] * 9 + [IN_HBM] * len(last),
            scratch=[
                pltpu.VMEM((2, 4 * width, token_count), bf16),
                pltpu.VMEM((2, rank, 4 * width), bf16),
                pltpu.SemaphoreType.DMA((2,)),
            ],
            out_specs=IN_HBM,
            aliases=aliases,
            flops=GRAD_FLOPS,
        )(facts, back_chosen, *pieces, *last)
    return mixed.T, grad_in, grad_out


def partner_shifts(count):
    return [[(i, i ^ k) for i in range(count)] for k in range(1, count)]


def gather_pieces(piece, axis):
    count = lax.axis_size(axis)
    if count & (count - 1) or count > 8:
        return lax.all_gather(piece, axis)
    me = lax.axis_index(axis)
    whole = jnp.zeros((count,) + piece.shape, piece.dtype)
    whole = lax.dynamic_update_index_in_dim(whole, piece, me, 0)
    for k, pairs in enumerate(partner_shifts(count), 1):
        arrived = lax.ppermute(piece, axis, pairs)
        whole = lax.dynamic_update_index_in_dim(whole, arrived, me ^ k, 0)
    return whole


def exchange_sum(pieces, axis):
    count = lax.axis_size(axis)
    if count & (count - 1) or count > 8:
        arrived = lax.all_to_all(pieces, axis, split_axis=0, concat_axis=0, tiled=True)
        return arrived.astype(jnp.float32).sum(0)
    me = lax.axis_index(axis)
    total = lax.dynamic_index_in_dim(pieces, me, 0, keepdims=False).astype(jnp.float32)
    for k, pairs in enumerate(partner_shifts(count), 1):
        leaving = lax.dynamic_index_in_dim(pieces, me ^ k, 0, keepdims=False)
        total = total + lax.ppermute(leaving, axis, pairs).astype(jnp.float32)
    return total


def pair_gather(piece):
    count = lax.axis_size("tensor")
    if count != 2:
        return lax.all_gather(piece, "tensor")
    other = lax.ppermute(piece, "tensor", [(0, 1), (1, 0)])
    mine_first = lax.axis_index("tensor") == 0
    return jnp.stack([jnp.where(mine_first, piece, other), jnp.where(mine_first, other, piece)])


def on_any_mesh(
    tokens,
    gate_weight,
    up_weight,
    down_weight,
    adapter_in,
    adapter_out,
    cotangent,
    block_owner,
    block_length,
    placement,
):
    f32, bf16 = jnp.float32, jnp.bfloat16
    batch_count, tensor_count = lax.axis_size("batch"), lax.axis_size("tensor")
    core = lax.axis_index("tensor")
    width = gate_weight.shape[1]
    model_width = gate_weight.shape[0]
    columns = cotangent.shape[1]
    token_count = cotangent.shape[0]
    block_count = block_owner.shape[0]
    block_size = token_count // block_count
    rank = adapter_in.shape[1]

    token_block = lax.broadcasted_iota(jnp.int32, (block_count, block_size), 0).reshape(-1)
    position = lax.broadcasted_iota(jnp.int32, (block_count, block_size), 1).reshape(-1)
    token_owner = jnp.repeat(block_owner, block_size)
    live = position < jnp.repeat(block_length, block_size)
    own_block = lax.broadcasted_iota(jnp.int32, (block_count, 1, 1), 0) == token_block

    def in_rank_space(matrices, features):
        every = jnp.dot(
            matrices.reshape(block_count * rank, -1), features, preferred_element_type=f32
        )
        return jnp.where(own_block, every.reshape(block_count, rank, token_count), 0.0).sum(0)

    in_blocks = adapter_in[block_owner]
    out_blocks = adapter_out[block_owner]
    cot_t = cotangent.T
    half = gather_pieces(tokens, "batch").reshape(token_count, -1)
    halves = pair_gather(half)
    rows = jnp.concatenate([halves[c] for c in range(tensor_count)], axis=1)

    back_part = jnp.where(live, in_rank_space(out_blocks, cot_t), 0.0).astype(bf16)
    cot_all = gather_pieces(cot_t, "batch")

    def weights_first(weight, values):
        return lax.dot_general(
            weight, values, (((0,), (1,)), ((), ())), preferred_element_type=f32
        )

    gate_value = weights_first(gate_weight, rows)
    up_value = weights_first(up_weight, rows)
    hidden = (jax.nn.silu(gate_value) * up_value).astype(bf16)
    hidden_all = gather_pieces(hidden, "batch")

    low_part = in_rank_space(in_blocks, hidden)
    base_part = lax.dot_general(
        down_weight, hidden, (((0,), (0,)), ((), ())), preferred_element_type=f32
    ).astype(bf16)
    base_part = base_part.reshape(batch_count, tensor_count, columns, token_count)
    ranked = jnp.concatenate([low_part.astype(bf16), back_part], axis=0)
    if tensor_count == 2:
        leaving = lax.dynamic_index_in_dim(base_part, 1 - core, 1, keepdims=False)
        kept = lax.dynamic_index_in_dim(base_part, core, 1, keepdims=False)
        arrived, ranked_other = lax.ppermute((leaving, ranked), "tensor", [(0, 1), (1, 0)])
        chip_base = (kept.astype(f32) + arrived.astype(f32)).astype(bf16)
        chip_ranked = (ranked.astype(f32) + ranked_other.astype(f32)).astype(bf16)
    else:
        chip_base = lax.psum_scatter(base_part, "tensor", scatter_dimension=1)
        chip_ranked = lax.psum(ranked, "tensor")
    leaving = jnp.concatenate(
        [chip_base, jnp.broadcast_to(chip_ranked, (batch_count,) + chip_ranked.shape)], axis=1
    )
    total = exchange_sum(leaving, "batch")
    base_sum = total[:columns]
    low = total[columns : columns + rank].astype(bf16)
    back = total[columns + rank :].astype(bf16)

    spread = jnp.where(own_block, low[None], jnp.zeros((), bf16)).reshape(-1, token_count)
    contribution = lax.dot_general(
        out_blocks.reshape(block_count * rank, columns),
        spread,
        (((0,), (0,)), ((), ())),
        preferred_element_type=f32,
    )
    mixed = (base_sum + lowrank_adapter_scale * contribution).astype(bf16).T

    slot = lax.axis_index(("batch", "tensor"))
    owner = placement[slot]
    count = jnp.where(block_owner == owner, block_length, 0).sum().astype(f32)
    coefficient = lowrank_adapter_scale / jnp.maximum(count, 1.0)
    chosen = token_owner == owner
    low_chosen = jnp.where(chosen & live, low, jnp.zeros((), bf16))
    back_chosen = jnp.where(chosen, back, jnp.zeros((), bf16))

    def slot_grad(ranked_values, pieces):
        both = pair_gather(pieces)
        features = jnp.swapaxes(both, 0, 1).reshape(-1, token_count)
        grad = lax.dot_general(
            ranked_values, features, (((1,), (1,)), ((), ())), preferred_element_type=f32
        )
        return (coefficient * grad).astype(bf16)[None]

    return mixed, slot_grad(back_chosen, hidden_all), slot_grad(low_chosen, cot_all)


def solution(mesh):
    placed = (
        P(("groups", "batch"), "tensor"),
        P(None, ("batch", "tensor")),
        P(None, ("batch", "tensor")),
        P(("batch", "tensor"), None),
        P("groups", None, ("batch", "tensor")),
        P("groups", None, ("batch", "tensor")),
        P("groups", ("batch", "tensor")),
        P("groups"),
        P("groups"),
        P("groups"),
    )
    on_device = on_any_mesh
    if mesh.shape["batch"] == 8 and mesh.shape["tensor"] == 2:
        on_device = on_chips
    return jax.shard_map(
        on_device,
        mesh=mesh,
        in_specs=placed,
        out_specs=(
            P("groups", ("batch", "tensor")),
            P(("groups", "batch", "tensor"), None, None),
            P(("groups", "batch", "tensor"), None, None),
        ),
        check_vma=False,
    )
```

```python
import functools

import jax
import jax.numpy as jnp
from jax import lax
from jax.experimental import pallas as pl
from jax.experimental.pallas import tpu as pltpu
from jax.sharding import PartitionSpec as P

lowrank_adapter_scale = 2.0

ROWS_BY_ROWS = (((1,), (1,)), ((), ()))
ASSEMBLE_FLOPS = 0
FIRST_FLOPS = 20000000000
LAST_FLOPS = 20000000000
FINAL_FLOPS = 8000000000
ADD_FLOPS = 0
PAIR_FLOPS = 0
SPLIT_FLOPS = 0
IN_VMEM = pl.BlockSpec(memory_space=pltpu.VMEM)
IN_HBM = pl.BlockSpec(memory_space=pl.ANY)
IN_SMEM = pl.BlockSpec(memory_space=pltpu.SMEM)


def kernel_call(
    body, out_shape, in_specs, scratch=(), out_specs=None, limit=16, aliases=None, flops=0
):
    return pl.pallas_call(
        body,
        out_shape=out_shape,
        in_specs=in_specs,
        out_specs=jax.tree.map(lambda _: IN_VMEM, out_shape) if out_specs is None else out_specs,
        scratch_shapes=list(scratch),
        input_output_aliases=aliases or {},
        compiler_params=pltpu.CompilerParams(vmem_limit_bytes=limit << 20),
        cost_estimate=pl.CostEstimate(flops=flops, bytes_accessed=0, transcendentals=0),
    )


class Facts:
    def __init__(self, ref):
        self.ref = ref
        self.blocks = (ref.shape[0] - 3) // 2
        self.batch, self.core, self.slot_owner = ref[0], ref[1], ref[2]

    def owner(self, block):
        return self.ref[3 + block]

    def length(self, block):
        return self.ref[3 + self.blocks + block]

    def lanes(self, token_count):
        lane = lax.broadcasted_iota(jnp.int32, (1, token_count), 1)
        size = token_count // self.blocks
        return lane, size, [(lane >= b * size) & (lane < (b + 1) * size) for b in range(self.blocks)]

    def live(self, token_count):
        lane, size, blocks = self.lanes(token_count)
        live = lane < 0
        for b in range(self.blocks):
            live = live | (blocks[b] & (lane < b * size + self.length(b)))
        return live

    def chosen(self, token_count):
        lane, _, blocks = self.lanes(token_count)
        chosen = lane < 0
        for b in range(self.blocks):
            mine = jnp.where(self.owner(b) == self.slot_owner, token_count, 0)
            chosen = chosen | (blocks[b] & (lane < mine))
        return chosen

    def coefficient(self):
        count = jnp.int32(0)
        for b in range(self.blocks):
            count = count + jnp.where(self.owner(b) == self.slot_owner, self.length(b), 0)
        return lowrank_adapter_scale / jnp.maximum(count, 1).astype(jnp.float32)


def prepare_body(owner, length, placement, adapter_out, adapter_in, cot, piece, *refs):
    facts, cot_and_back, out_blocks, in_blocks, passed, sems = refs
    passed[...] = piece[...]
    block_count = owner.shape[0]
    facts[0], facts[1] = lax.axis_index("batch"), lax.axis_index("tensor")
    facts[2] = placement[lax.axis_index("batch") * 2 + lax.axis_index("tensor")]
    for b in range(block_count):
        facts[3 + b] = owner[b]
        facts[3 + block_count + b] = length[b]
    facts = Facts(facts)
    copies = []
    for b in range(facts.blocks):
        for i, (source, target) in enumerate(((adapter_out, out_blocks), (adapter_in, in_blocks))):
            copies.append(
                pltpu.make_async_copy(source.at[facts.owner(b)], target.at[b], sems.at[i, b])
            )
    for copy in copies:
        copy.start()
    columns, token_count = cot.shape
    for b in range(cot_and_back.shape[0]):
        cot_and_back[b, :columns] = cot[...]
    for copy in copies:
        copy.wait()
    _, _, blocks = facts.lanes(token_count)
    total = jnp.zeros((out_blocks.shape[1], token_count), jnp.float32)
    for b in range(facts.blocks):
        every = jnp.dot(out_blocks[b], cot[...], preferred_element_type=jnp.float32)
        total = jnp.where(blocks[b], every, total)
    total = jnp.where(facts.live(token_count), total, 0.0)
    for b in range(cot_and_back.shape[0]):
        cot_and_back[b, columns:] = total.astype(cot_and_back.dtype)


def run_copies(pairs, sems):
    copies = [
        pltpu.make_async_copy(source, target, sems.at[i])
        for i, (source, target) in enumerate(pairs)
    ]
    for copy in copies:
        copy.start()
    for copy in copies:
        copy.wait()


def assemble_body(*refs):
    pieces, out = refs[:-1], refs[-1]
    batch, own_core = lax.axis_index("batch"), lax.axis_index("tensor")
    count = len(pieces) // 2
    rows, half = pieces[0].shape
    for i, piece in enumerate(pieces):
        row = pl.multiple_of((batch ^ (i % count)) * rows, rows)
        core = own_core if i < count else 1 - own_core
        out[pl.ds(row, rows), pl.ds(pl.multiple_of(core * half, 128), half)] = piece[...]


def split_body(facts, base, hidden, in_blocks, *refs):
    facts, kept, leaving = Facts(facts), refs[-2], refs[-1]
    token_count = base.shape[0]
    rank = in_blocks.shape[1]
    columns = (kept.shape[0] - rank) // 8
    for b in range(8):
        both = base[:, b * 2 * columns : (b + 1) * 2 * columns].astype(jnp.float32).T
        both = both.astype(kept.dtype)
        here = pl.ds(b * columns, columns)

        @pl.when(facts.core == 0)
        def _():
            kept[here] = both[:columns]
            leaving[here] = both[columns:]

        @pl.when(facts.core != 0)
        def _():
            kept[here] = both[columns:]
            leaving[here] = both[:columns]

    _, _, blocks = facts.lanes(token_count)
    low = jnp.zeros((rank, token_count), jnp.float32)
    for b in range(facts.blocks):
        every = jnp.dot(in_blocks[b], hidden[...], preferred_element_type=jnp.float32)
        low = jnp.where(blocks[b], every, low)
    tail = pl.ds(8 * columns, rank)
    kept[tail] = low.astype(kept.dtype)
    leaving[tail] = low.astype(kept.dtype)


def add_body(facts, kept, arrived, own, leaving):
    rank = own.shape[0] - (kept.shape[0] - own.shape[0])
    columns = (own.shape[0] - rank) // 4
    side = Facts(facts).batch % 2

    def added(first, count):
        here = pl.ds(first, count)
        total = kept[here].astype(jnp.float32) + arrived[here].astype(jnp.float32)
        return total.astype(own.dtype)

    for z in range(4):
        here = pl.ds(z * columns, columns)
        own[here] = added(pl.multiple_of((2 * z + side) * columns, 16), columns)
        leaving[here] = added(pl.multiple_of((2 * z + 1 - side) * columns, 16), columns)
    low = added(8 * columns, rank)
    own[4 * columns :] = low
    leaving[4 * columns :] = low


def add_pair_body(facts, own, arrived, *refs):
    outs = refs[-4:]
    columns = (own.shape[0] - outs[0].shape[0]) // 3
    place = Facts(facts).batch // 2

    def added(first, count):
        here = pl.ds(first, count)
        total = own[here].astype(jnp.float32) + arrived[here].astype(jnp.float32)
        return total.astype(own.dtype)

    low = added(4 * columns, own.shape[0] - 4 * columns)
    for flip, out in enumerate(outs):
        out[:columns] = added(pl.multiple_of((place ^ flip) * columns, 16), columns)
        out[columns:] = low


def final_body(facts, out_blocks, features, *refs):
    facts, arrived, (mixed, grad, ranked) = Facts(facts), refs[:-3], refs[-3:]
    columns, token_count = mixed.shape
    total = arrived[0][...].astype(jnp.float32)
    for share in arrived[1:]:
        total = total + share[...].astype(jnp.float32)
    low = total[columns:]
    _, _, blocks = facts.lanes(token_count)
    contribution = jnp.zeros(mixed.shape, jnp.float32)
    for b in range(facts.blocks):
        every = lax.dot_general(
            out_blocks[b],
            low.astype(jnp.bfloat16),
            (((0,), (0,)), ((), ())),
            preferred_element_type=jnp.float32,
        )
        contribution = jnp.where(blocks[b], every, contribution)
    mixed[...] = (total[:columns] + lowrank_adapter_scale * contribution).astype(mixed.dtype)
    chosen = facts.chosen(token_count) & facts.live(token_count)
    ranked[...] = jnp.where(chosen, low, 0.0).astype(ranked.dtype)
    total = lax.dot_general(
        ranked[...], features[...], ROWS_BY_ROWS, preferred_element_type=jnp.float32
    )
    grad[0] = (facts.coefficient() * total).astype(grad.dtype)


def copy_body(source, _, target):
    target[...] = source[...]


def pass_body(*refs):
    pass


def back_body(facts, gathered, gathered_other, features, ranked):
    back = jnp.zeros(ranked.shape, jnp.float32)
    first = gathered.shape[1] - ranked.shape[0]
    for pieces in (gathered, gathered_other):
        for b in range(pieces.shape[0]):
            back = back + pieces[b, first:].astype(jnp.float32)
    facts = Facts(facts)
    chosen = facts.chosen(ranked.shape[1])
    ranked[...] = jnp.where(chosen, back, 0.0).astype(ranked.dtype)
    for half, pieces in ((facts.core, gathered), (1 - facts.core, gathered_other)):
        for b in range(pieces.shape[0]):
            here = pl.ds(pl.multiple_of((2 * b + half) * first, 16), first)
            features[here] = pieces[b, :first]


def in_grad_body(facts, ranked, *refs, flips):
    pieces, (out, features, result, sems) = refs[:8], refs[-4:]
    facts = Facts(facts)
    rows = pieces[0].shape[0]
    side = facts.batch % 2
    factor = facts.coefficient()
    leaving = []
    for i, flip in enumerate(flips):
        for j in range(4):
            y = side if j < 2 else 1 - side
            core = facts.core if j % 2 == 0 else 1 - facts.core
            here = pl.ds(pl.multiple_of((y * 2 + core) * rows, 16), rows)
            features[i, here] = pieces[4 * i + j][...]
        total = lax.dot_general(
            ranked[...], features[i], ROWS_BY_ROWS, preferred_element_type=jnp.float32
        )
        result[i] = (factor * total).astype(result.dtype)
        columns = 4 * rows
        first = ((facts.batch ^ flip) // 2) * columns
        target = out.at[0, :, pl.ds(pl.multiple_of(first, 128), columns)]
        leaving.append(pltpu.make_async_copy(result.at[i], target, sems.at[i]))
        leaving[-1].start()
    for copy in leaving:
        copy.wait()


def on_chips(
    tokens,
    gate_weight,
    up_weight,
    down_weight,
    adapter_in,
    adapter_out,
    cotangent,
    block_owner,
    block_length,
    placement,
):
    f32, bf16 = jnp.float32, jnp.bfloat16
    width = gate_weight.shape[1]
    model_width = gate_weight.shape[0]
    token_count, columns = cotangent.shape
    rank = adapter_in.shape[1]
    block_count = block_owner.shape[0]
    def array(*shape):
        return jax.ShapeDtypeStruct(shape, bf16)

    def flip(piece, k):
        return lax.ppermute(piece, "batch", [(i, i ^ k) for i in range(8)])

    def to_other_core(piece):
        return lax.ppermute(piece, "tensor", [(0, 1), (1, 0)])

    def along_z(piece):
        return {0: piece, **{k: flip(piece, k) for k in (2, 4, 6)}}

    def then_along_y(line):
        return [line[k] if k in line else flip(line[k ^ 1], 1) for k in range(8)]

    line = along_z(tokens)
    arrived = line[2]
    facts, cot_and_back, out_blocks, in_blocks, line[2] = kernel_call(
        prepare_body,
        [
            jax.ShapeDtypeStruct((3 + 2 * block_count,), jnp.int32),
            array(8, columns + rank, token_count),
            array(block_count, rank, columns),
            array(block_count, rank, width),
            array(*tokens.shape),
        ],
        [IN_SMEM] * 3 + [IN_HBM, IN_HBM, IN_VMEM, IN_VMEM],
        out_specs=[IN_SMEM] + [IN_VMEM] * 4,
        scratch=[pltpu.SemaphoreType.DMA((2, block_count))],
        limit=56,
    )(block_owner, block_length, placement, adapter_out, adapter_in, cotangent.T, line[2])
    own = then_along_y(line)
    other = [to_other_core(piece) for piece in own]
    gathered = lax.all_to_all(
        cot_and_back, "batch", split_axis=0, concat_axis=0, tiled=True
    )
    rows = kernel_call(
        assemble_body,
        array(token_count, model_width),
        [IN_VMEM] * 16,
        flops=ASSEMBLE_FLOPS,
    )(*own[:2], arrived, *own[3:], *other)
    gate_value = lax.dot_general(gate_weight.T, rows, ROWS_BY_ROWS, preferred_element_type=f32)
    up_value = lax.dot_general(up_weight.T, rows, ROWS_BY_ROWS, preferred_element_type=f32)
    hidden = (jax.nn.silu(gate_value) * up_value).astype(bf16)
    base_part = lax.dot_general(
        hidden, down_weight, (((0,), (0,)), ((), ())), preferred_element_type=f32
    ).astype(bf16)
    kept, leaving = kernel_call(
        split_body,
        [array(8 * columns + rank, token_count)] * 2,
        [IN_SMEM] + [IN_VMEM] * 3,
        flops=SPLIT_FLOPS,
    )(facts, base_part, hidden, in_blocks)
    stays, leaving = kernel_call(
        add_body,
        [array(4 * columns + rank, token_count)] * 2,
        [IN_SMEM] + [IN_VMEM] * 2,
        flops=ADD_FLOPS,
    )(facts, kept, to_other_core(leaving))
    line = along_z(hidden)
    line[0] = kernel_call(copy_body, array(width, token_count), [IN_VMEM, IN_HBM])(
        hidden, line[2]
    )
    gathered = kernel_call(
        pass_body,
        array(8, columns + rank, token_count),
        [IN_HBM] * 2,
        out_specs=IN_HBM,
        aliases={0: 0},
    )(gathered, stays)
    gathered_other = to_other_core(gathered)
    hidden_own = then_along_y(line)
    hidden_other = [to_other_core(piece) for piece in hidden_own]
    shares = kernel_call(
        add_pair_body,
        [array(columns + rank, token_count)] * 4,
        [IN_SMEM] + [IN_VMEM] * 2 + [IN_HBM] * 3,
        flops=PAIR_FLOPS,
    )(facts, stays, flip(leaving, 1), line[2], line[2], line[2])
    shares = [shares[0]] + [flip(shares[z], 2 * z) for z in (1, 2, 3)]
    cot_all, back_chosen = kernel_call(
        back_body,
        [array(model_width, token_count), array(rank, token_count)],
        [IN_SMEM] + [IN_VMEM] * 2,
    )(facts, gathered, gathered_other)
    mixed, grad_out, low_chosen = kernel_call(
        final_body,
        [array(columns, token_count), array(1, rank, model_width), array(rank, token_count)],
        [IN_SMEM] + [IN_VMEM] * 6,
        flops=FINAL_FLOPS,
    )(facts, out_blocks, cot_all, *shares)
    grad_in = None
    for flips in ((0, 2), (4, 6)):
        order = [p for k in flips for p in (k, k ^ 1)]
        pieces = [p for k in order for p in (hidden_own[k], hidden_other[k])]
        if grad_in is None:
            last, aliases = [], {}
        else:
            last, aliases = [grad_in, low_chosen], {10: 0}
        grad_in = kernel_call(
            functools.partial(in_grad_body, flips=flips),
            array(1, rank, 16 * width),
            [IN_SMEM] + [IN_VMEM] * 9 + [IN_HBM] * len(last),
            scratch=[
                pltpu.VMEM((2, 4 * width, token_count), bf16),
                pltpu.VMEM((2, rank, 4 * width), bf16),
                pltpu.SemaphoreType.DMA((2,)),
            ],
            out_specs=IN_HBM,
            aliases=aliases,
            flops=LAST_FLOPS if last else FIRST_FLOPS,
        )(facts, back_chosen, *pieces, *last)
    return mixed.T, grad_in, grad_out


def partner_shifts(count):
    return [[(i, i ^ k) for i in range(count)] for k in range(1, count)]


def gather_pieces(piece, axis):
    count = lax.axis_size(axis)
    if count & (count - 1) or count > 8:
        return lax.all_gather(piece, axis)
    me = lax.axis_index(axis)
    whole = jnp.zeros((count,) + piece.shape, piece.dtype)
    whole = lax.dynamic_update_index_in_dim(whole, piece, me, 0)
    for k, pairs in enumerate(partner_shifts(count), 1):
        arrived = lax.ppermute(piece, axis, pairs)
        whole = lax.dynamic_update_index_in_dim(whole, arrived, me ^ k, 0)
    return whole


def exchange_sum(pieces, axis):
    count = lax.axis_size(axis)
    if count & (count - 1) or count > 8:
        arrived = lax.all_to_all(pieces, axis, split_axis=0, concat_axis=0, tiled=True)
        return arrived.astype(jnp.float32).sum(0)
    me = lax.axis_index(axis)
    total = lax.dynamic_index_in_dim(pieces, me, 0, keepdims=False).astype(jnp.float32)
    for k, pairs in enumerate(partner_shifts(count), 1):
        leaving = lax.dynamic_index_in_dim(pieces, me ^ k, 0, keepdims=False)
        total = total + lax.ppermute(leaving, axis, pairs).astype(jnp.float32)
    return total


def pair_gather(piece):
    count = lax.axis_size("tensor")
    if count != 2:
        return lax.all_gather(piece, "tensor")
    other = lax.ppermute(piece, "tensor", [(0, 1), (1, 0)])
    mine_first = lax.axis_index("tensor") == 0
    return jnp.stack([jnp.where(mine_first, piece, other), jnp.where(mine_first, other, piece)])


def on_any_mesh(
    tokens,
    gate_weight,
    up_weight,
    down_weight,
    adapter_in,
    adapter_out,
    cotangent,
    block_owner,
    block_length,
    placement,
):
    f32, bf16 = jnp.float32, jnp.bfloat16
    batch_count, tensor_count = lax.axis_size("batch"), lax.axis_size("tensor")
    core = lax.axis_index("tensor")
    width = gate_weight.shape[1]
    model_width = gate_weight.shape[0]
    columns = cotangent.shape[1]
    token_count = cotangent.shape[0]
    block_count = block_owner.shape[0]
    block_size = token_count // block_count
    rank = adapter_in.shape[1]

    token_block = lax.broadcasted_iota(jnp.int32, (block_count, block_size), 0).reshape(-1)
    position = lax.broadcasted_iota(jnp.int32, (block_count, block_size), 1).reshape(-1)
    token_owner = jnp.repeat(block_owner, block_size)
    live = position < jnp.repeat(block_length, block_size)
    own_block = lax.broadcasted_iota(jnp.int32, (block_count, 1, 1), 0) == token_block

    def in_rank_space(matrices, features):
        every = jnp.dot(
            matrices.reshape(block_count * rank, -1), features, preferred_element_type=f32
        )
        return jnp.where(own_block, every.reshape(block_count, rank, token_count), 0.0).sum(0)

    in_blocks = adapter_in[block_owner]
    out_blocks = adapter_out[block_owner]
    cot_t = cotangent.T
    half = gather_pieces(tokens, "batch").reshape(token_count, -1)
    halves = pair_gather(half)
    rows = jnp.concatenate([halves[c] for c in range(tensor_count)], axis=1)

    back_part = jnp.where(live, in_rank_space(out_blocks, cot_t), 0.0).astype(bf16)
    cot_all = gather_pieces(cot_t, "batch")

    def weights_first(weight, values):
        return lax.dot_general(
            weight, values, (((0,), (1,)), ((), ())), preferred_element_type=f32
        )

    gate_value = weights_first(gate_weight, rows)
    up_value = weights_first(up_weight, rows)
    hidden = (jax.nn.silu(gate_value) * up_value).astype(bf16)
    hidden_all = gather_pieces(hidden, "batch")

    low_part = in_rank_space(in_blocks, hidden)
    base_part = lax.dot_general(
        down_weight, hidden, (((0,), (0,)), ((), ())), preferred_element_type=f32
    ).astype(bf16)
    base_part = base_part.reshape(batch_count, tensor_count, columns, token_count)
    ranked = jnp.concatenate([low_part.astype(bf16), back_part], axis=0)
    if tensor_count == 2:
        leaving = lax.dynamic_index_in_dim(base_part, 1 - core, 1, keepdims=False)
        kept = lax.dynamic_index_in_dim(base_part, core, 1, keepdims=False)
        arrived, ranked_other = lax.ppermute((leaving, ranked), "tensor", [(0, 1), (1, 0)])
        chip_base = (kept.astype(f32) + arrived.astype(f32)).astype(bf16)
        chip_ranked = (ranked.astype(f32) + ranked_other.astype(f32)).astype(bf16)
    else:
        chip_base = lax.psum_scatter(base_part, "tensor", scatter_dimension=1)
        chip_ranked = lax.psum(ranked, "tensor")
    leaving = jnp.concatenate(
        [chip_base, jnp.broadcast_to(chip_ranked, (batch_count,) + chip_ranked.shape)], axis=1
    )
    total = exchange_sum(leaving, "batch")
    base_sum = total[:columns]
    low = total[columns : columns + rank].astype(bf16)
    back = total[columns + rank :].astype(bf16)

    spread = jnp.where(own_block, low[None], jnp.zeros((), bf16)).reshape(-1, token_count)
    contribution = lax.dot_general(
        out_blocks.reshape(block_count * rank, columns),
        spread,
        (((0,), (0,)), ((), ())),
        preferred_element_type=f32,
    )
    mixed = (base_sum + lowrank_adapter_scale * contribution).astype(bf16).T

    slot = lax.axis_index(("batch", "tensor"))
    owner = placement[slot]
    count = jnp.where(block_owner == owner, block_length, 0).sum().astype(f32)
    coefficient = lowrank_adapter_scale / jnp.maximum(count, 1.0)
    chosen = token_owner == owner
    low_chosen = jnp.where(chosen & live, low, jnp.zeros((), bf16))
    back_chosen = jnp.where(chosen, back, jnp.zeros((), bf16))

    def slot_grad(ranked_values, pieces):
        both = pair_gather(pieces)
        features = jnp.swapaxes(both, 0, 1).reshape(-1, token_count)
        grad = lax.dot_general(
            ranked_values, features, (((1,), (1,)), ((), ())), preferred_element_type=f32
        )
        return (coefficient * grad).astype(bf16)[None]

    return mixed, slot_grad(back_chosen, hidden_all), slot_grad(low_chosen, cot_all)


def solution(mesh):
    placed = (
        P(("groups", "batch"), "tensor"),
        P(None, ("batch", "tensor")),
        P(None, ("batch", "tensor")),
        P(("batch", "tensor"), None),
        P("groups", None, ("batch", "tensor")),
        P("groups", None, ("batch", "tensor")),
        P("groups", ("batch", "tensor")),
        P("groups"),
        P("groups"),
        P("groups"),
    )
    on_device = on_any_mesh
    if mesh.shape["batch"] == 8 and mesh.shape["tensor"] == 2:
        on_device = on_chips
    return jax.shard_map(
        on_device,
        mesh=mesh,
        in_specs=placed,
        out_specs=(
            P("groups", ("batch", "tensor")),
            P(("groups", "batch", "tensor"), None, None),
            P(("groups", "batch", "tensor"), None, None),
        ),
        check_vma=False,
    )
```
